512 devices in a mesh: pool: 64 (over x, y, core), tp: 8 (over z).
Axes of the slice: x: 4, y: 8, z: 8, core: 2. Of those that a mesh axis runs over, the one named last changes fastest.
Arguments:
- queries: bfloat16 [64, 6144], P('pool', 'tp'), may hold values from -6 to 6
- suffix_keys: bfloat16 [64, 1024], P('pool', 'tp'), may hold values from -15 to 15
- suffix_values: bfloat16 [64, 1024], P('pool', 'tp'), may hold values from -6 to 6
- prefix_keys: bfloat16 [1024, 128, 1024], P('pool', None, 'tp'), may hold values from -16 to 16
- prefix_values: bfloat16 [1024, 128, 1024], P('pool', None, 'tp'), may hold values from -6 to 6
- block_slot: int32 [2, 256], replicated, may hold values from 0 to 1023, as said below
- suffix_len: int32 [2], replicated, may hold values from 8 to 32, as said below
- out_weight: bfloat16 [6144, 12288], P('tp', 'pool'), may hold values from -0.078125 to 0.078125
Outputs:
- attn_out: bfloat16 [64, 12288], P('tp', 'pool')
The draws below stay inside these ranges and needn't reach their ends.
Inputs may be any that keep to these rules, and one draw needn't show every extreme that they name: `block_slot`: the 512 entries are distinct slots owner * 16 + k; the blocks of each owner fill its slots k = 0 to its count - 1, counts differ between owners, and some owners have all 16 slots in use. `suffix_len`: some conversation has all 32 positions live.
All inputs are finite; a program needn't handle non-finite values.
Results may differ from the reference program's by a relative error of at most 0.019.
Values may be sent and summed in bfloat16 or wider, within the bound.
A program may use at most 64 MiB of HBM per device.

```python
import math
import jax
import jax.numpy as jnp
from jax import lax

D = 12288
H = 48
KVH = 8
HD = 128
CONV = 2
SUF = 32
BLK_DEV = 8
BLOCK = 128
OWNERS = 64
CAP = 16
SLOTS = 1024
NBLK = 256
TOKENS = 64


def draw_queries(key, part):
    key = jax.random.fold_in(key, 11)
    return jnp.clip(jax.random.normal(key, (TOKENS, H * HD), jnp.float32), -6.0, 6.0).astype(jnp.bfloat16)


def draw_suffix_keys(key, part):
    key = jax.random.fold_in(key, 12)
    return jnp.clip(3.0 * jax.random.normal(key, (TOKENS, KVH * HD), jnp.float32), -15.0, 15.0).astype(jnp.bfloat16)


def draw_block_slot(key, part):
    key = jax.random.fold_in(key, 21)
    first_key, second_key, third_key = jax.random.split(key, 3)
    order = jax.random.permutation(first_key, OWNERS)
    shifts = jax.random.randint(second_key, (OWNERS // 2,), 0, BLK_DEV + 1)
    shifts = shifts.at[0].set(BLK_DEV).at[1].set(BLK_DEV)
    ranked = jnp.concatenate([BLK_DEV + shifts, BLK_DEV - shifts]).astype(jnp.int32)
    counts = jnp.zeros((OWNERS,), jnp.int32).at[order].set(ranked)
    last_count = counts[OWNERS - 1]
    counts = counts.at[order[1]].set(last_count).at[OWNERS - 1].set(CAP).astype(jnp.int32)
    used = jnp.arange(CAP, dtype=jnp.int32)[None, :] < counts[:, None]
    free_rank = jnp.where(used.reshape(-1), 0, 1).astype(jnp.int32)
    filled = jnp.argsort(free_rank, stable=True)[:CONV * NBLK].astype(jnp.int32)
    spread = jax.random.permutation(third_key, CONV * NBLK)
    return filled[spread].astype(jnp.int32).reshape(CONV, NBLK)


def draw_suffix_len(key, part):
    key = jax.random.fold_in(key, 31)
    first_key, second_key = jax.random.split(key, 2)
    lengths = jax.random.randint(first_key, (CONV,), SUF // 4, SUF + 1)
    full_one = jax.random.randint(second_key, (), 0, CONV)
    return jnp.where(jnp.arange(CONV) == full_one, SUF, lengths).astype(jnp.int32)


def steps_of(own_key, extent, cuts, smallest, largest):
    factor_of, own = 1.0, jax.random.fold_in(own_key, 6)
    for axis_at, shards_of in cuts:
        heights = jnp.exp(jax.random.uniform(jax.random.fold_in(own, axis_at), (shards_of,), jnp.float32, smallest / len(cuts), largest / len(cuts)))
        factor_of = factor_of * jnp.repeat(heights, extent[axis_at] // shards_of).reshape([-1 if axis == axis_at else 1 for axis in range(len(extent))])
    return factor_of


def scatter_about(own_key, shape, scale, limit, cuts=(), kind=jnp.bfloat16):
    values = jax.random.normal(own_key, shape, jnp.float32) * scale
    if len(cuts) > 0:
        values = steps_of(own_key, shape, cuts, -0.22, 0.18) * values
    return jnp.clip(values, min=-limit, max=limit).astype(kind)


def setup_inputs(seed: int = 0) -> dict:
    streams_of = jax.random.split(jax.random.key(seed), 9)
    queries = draw_queries(jax.random.fold_in(streams_of[8], 71), 0)
    suffix_keys = draw_suffix_keys(jax.random.fold_in(streams_of[8], 71), 0)
    suffix_values = scatter_about(streams_of[2], (TOKENS, KVH * HD), 1.0, 6.0, ((0, 64), (1, 8)))
    prefix_keys = scatter_about(streams_of[3], (SLOTS, BLOCK, KVH * HD), 3.0, 16.0, ((0, 64), (2, 8)))
    prefix_values = scatter_about(streams_of[4], (SLOTS, BLOCK, KVH * HD), 1.0, 6.0, ((0, 64), (2, 8)))
    block_slot = draw_block_slot(jax.random.fold_in(streams_of[8], 71), 0)
    suffix_len = draw_suffix_len(jax.random.fold_in(streams_of[8], 71), 0)
    out_weight = scatter_about(streams_of[7], (H * HD, D), (H * HD) ** -0.5, 0.078125, ((0, 8), (1, 64)))
    return dict(queries=queries, suffix_keys=suffix_keys, suffix_values=suffix_values, prefix_keys=prefix_keys, prefix_values=prefix_values, block_slot=block_slot, suffix_len=suffix_len, out_weight=out_weight)


NEG_FILL = -1e+30

def block_terms(query_rows, key_rows, value_rows, score_scale, allowed):
    scores = jnp.einsum('rnge,kne->rngk', query_rows.astype(jnp.float32), key_rows.astype(jnp.float32)) * score_scale
    if allowed is not None:
        scores = jnp.where(allowed, scores, NEG_FILL)
    block_max = lax.optimization_barrier(jnp.max(scores, axis=-1))
    powers = jnp.exp(scores - block_max[..., None])
    block_sum = lax.optimization_barrier(jnp.sum(powers, axis=-1))
    rounded = lax.optimization_barrier(powers.astype(jnp.bfloat16)).astype(jnp.float32)
    block_out = jnp.einsum('rngk,kne->rnge', rounded, value_rows.astype(jnp.float32))
    return (block_max, block_sum, block_out)

def join(earlier, later):
    row_max = jnp.maximum(earlier[0], later[0])
    early_scale = jnp.exp(earlier[0] - row_max)
    late_scale = jnp.exp(later[0] - row_max)
    row_total = early_scale * earlier[1] + late_scale * later[1]
    numerator = early_scale[..., None] * earlier[2] + late_scale[..., None] * later[2]
    return (row_max, row_total, numerator)

def reference(queries, suffix_keys, suffix_values, prefix_keys, prefix_values, block_slot, suffix_len, out_weight):
    groups = H // KVH
    score_scale = 1.0 / math.sqrt(HD)
    pieces = []
    for dialog in range(CONV):
        lower = dialog * SUF
        query_rows = queries[lower:lower + SUF].reshape(SUF, KVH, groups, HD)

        def visit(carry_state, slot_index):
            key_rows = lax.dynamic_index_in_dim(prefix_keys, slot_index, 0, keepdims=False).reshape(BLOCK, KVH, HD)
            value_rows = lax.dynamic_index_in_dim(prefix_values, slot_index, 0, keepdims=False).reshape(BLOCK, KVH, HD)
            return (join(carry_state, block_terms(query_rows, key_rows, value_rows, score_scale, None)), slot_index)
        start = (jnp.full((SUF, KVH, groups), NEG_FILL, jnp.float32), jnp.zeros((SUF, KVH, groups), jnp.float32), jnp.zeros((SUF, KVH, groups, HD), jnp.float32))
        carry_state, visited = lax.scan(visit, start, block_slot[dialog])
        own_keys = suffix_keys[lower:lower + SUF].reshape(SUF, KVH, HD)
        own_values = suffix_values[lower:lower + SUF].reshape(SUF, KVH, HD)
        positions = jnp.arange(SUF, dtype=jnp.int32)
        allowed = positions[None, :] <= positions[:, None]
        carry_state = join(carry_state, block_terms(query_rows, own_keys, own_values, score_scale, allowed[:, None, None, :]))
        values_out = carry_state[2] / carry_state[1][..., None]
        alive_rows = positions < suffix_len[dialog]
        shaped = jnp.where(alive_rows[:, None, None, None], values_out, 0.0)
        pieces.append(shaped.reshape(SUF, H * HD).astype(jnp.bfloat16))
    attention = jnp.concatenate(pieces, axis=0)
    return jnp.dot(attention, out_weight, preferred_element_type=jnp.float32).astype(jnp.bfloat16)
```

```python
import functools
import math

import jax
import jax.numpy as jnp
from jax import lax
from jax.experimental import pallas as pl
from jax.experimental.pallas import tpu as pltpu
from jax.sharding import PartitionSpec as P

H = 48
KVH = 8
HD = 128
CONV = 2
SUF = 32
GROUPS = H // KVH
ROWS = GROUPS * SUF
NEG = -1e30
EXP_SCALE = math.log2(math.e) / math.sqrt(HD)
MESH = pl.DeviceIdType.MESH

NX = 4
NY = 8
CHIPS = NX * NY
TP = 8
PAIRS = 16


def far_first(count, step):
    half = count // 2
    return half + (1 - 2 * lax.rem(step, 2)) * lax.div(step + 1, 2)


def kernel(
    q_ref, sk_ref, sv_ref, keys_ref, values_ref, slot_ref, len_ref, w_ref,
    out_ref,
    qmsg, qbuf, kbuf, vbuf, wbuf, bias, sbuf, smsg, rbuf, amsg, abuf, omsg, obuf,
    local_sem, part_send, part_recv, send_sem, recv_sem,
):
    pool = lax.axis_index("pool")
    tp = lax.axis_index("tp")
    core = lax.rem(pool, 2)
    chip = lax.div(pool, 2)
    x = lax.div(chip, NY)
    y = lax.rem(chip, NY)
    other = pool + 1 - 2 * core
    home = lax.div(x, NX // CONV)
    token = lax.rem(pool, SUF)

    def chip_at(step):
        to_x = lax.rem(x + far_first(NX, lax.rem(step, NX)), NX)
        to_y = lax.rem(y + far_first(NY, lax.div(step, NX)), NY)
        return to_x * NY + to_y

    local = [
        pltpu.make_async_copy(keys_ref, kbuf.at[pl.ds(0, PAIRS // 2)], local_sem.at[0]),
        pltpu.make_async_copy(values_ref, vbuf.at[pl.ds(0, PAIRS // 2)], local_sem.at[1]),
        pltpu.make_async_copy(w_ref, wbuf.at[core], local_sem.at[2]),
    ]
    for copy in local:
        copy.start()

    barrier = pltpu.get_barrier_semaphore()

    def greet(step, carry):
        to = chip_at(step)
        pl.semaphore_signal(barrier, inc=1, device_id=(to * 2 + core, tp), device_id_type=MESH)
        pl.semaphore_signal(barrier, inc=1, device_id=(to * 2 + 1 - core, tp), device_id_type=MESH)
        return carry

    lax.fori_loop(0, CHIPS - 1, greet, 0)

    def greet_tp(step, carry):
        to = lax.rem(tp + 1 + step, TP)
        pl.semaphore_signal(barrier, inc=1, device_id=(pool, to), device_id_type=MESH)
        pl.semaphore_signal(barrier, inc=1, device_id=(other, to), device_id_type=MESH)
        return carry

    lax.fori_loop(0, TP - 1, greet_tp, 0)
    pl.semaphore_signal(barrier, inc=1, device_id=(other, tp), device_id_type=MESH)

    rows = [q_ref[:, g * HD : (g + 1) * HD].astype(jnp.float32) for g in range(GROUPS)]
    rows += [sk_ref[...].astype(jnp.float32), sv_ref[...].astype(jnp.float32)]
    qmsg[...] = jnp.concatenate(rows, axis=0)

    slots = jnp.where(core == 0, slot_ref[0:1, :], slot_ref[1:2, :])
    pair = lax.broadcasted_iota(jnp.int32, (PAIRS, 1), 0)
    first = jnp.where(pair < PAIRS // 2, pool * PAIRS, other * PAIRS - PAIRS) + 2 * pair
    for side in range(2):
        found = jnp.max(jnp.where(slots == first + side, 1.0, 0.0), axis=1, keepdims=True)
        bias[:, side * HD : (side + 1) * HD] = jnp.broadcast_to(
            jnp.where(found > 0.5, 0.0, NEG), (PAIRS, HD)
        )

    pl.semaphore_wait(barrier, 2 * (CHIPS - 1) + 2 * (TP - 1) + 1)

    def send_queries(step, carry):
        to = chip_at(step) * 2 + home
        mine = qbuf.at[pl.ds(pl.multiple_of(token * 8, 8), 8)]

        @pl.when(to != pool)
        def _():
            pltpu.make_async_remote_copy(
                src_ref=qmsg, dst_ref=mine, send_sem=send_sem.at[0], recv_sem=recv_sem.at[0],
                device_id=(to, tp), device_id_type=MESH,
            ).start()

        @pl.when(to == pool)
        def _():
            pltpu.make_async_copy(qmsg, mine, recv_sem.at[0]).start()

        return carry

    lax.fori_loop(0, CHIPS, send_queries, 0)

    swaps = [
        pltpu.make_async_remote_copy(
            src_ref=src, dst_ref=dst, send_sem=part_send.at[n], recv_sem=part_recv.at[n],
            device_id=(other, tp), device_id_type=MESH,
        )
        for n, (src, dst) in enumerate(
            [
                (keys_ref, kbuf.at[pl.ds(PAIRS // 2, PAIRS // 2)]),
                (values_ref, vbuf.at[pl.ds(PAIRS // 2, PAIRS // 2)]),
                (w_ref, wbuf.at[core]),
            ]
        )
    ]
    for copy in swaps:
        copy.start()
    for copy in local:
        copy.wait()
    swaps[0].wait()
    swaps[1].wait()
    pltpu.make_async_copy(qbuf, qbuf, recv_sem.at[0]).wait()

    def head_rows(ref, row):
        return ref[pl.ds(row, SUF, stride=8), :]

    queries = jnp.concatenate([head_rows(qbuf, g) for g in range(GROUPS)], axis=0).astype(jnp.bfloat16)
    own_keys = head_rows(qbuf, 6).astype(jnp.bfloat16)
    own_values = head_rows(qbuf, 7).astype(jnp.bfloat16)
    contract = (((1,), (1,)), ((), ()))

    def score(r, top):
        s = lax.dot_general(queries, kbuf[r], contract, preferred_element_type=jnp.float32)
        s = s + bias[pl.ds(r, 1), :]
        sbuf[r] = s
        return jnp.maximum(top, jnp.maximum(s[:, :HD], s[:, HD:]))

    top = lax.fori_loop(0, PAIRS, score, jnp.full((ROWS, HD), NEG, jnp.float32), unroll=4)
    own = lax.dot_general(queries, own_keys, contract, preferred_element_type=jnp.float32)
    row_pos = lax.rem(lax.broadcasted_iota(jnp.int32, (ROWS, SUF), 0), SUF)
    key_pos = lax.broadcasted_iota(jnp.int32, (ROWS, SUF), 1)
    own = jnp.where((key_pos == chip) & (row_pos >= chip), own, NEG)
    row_max = jnp.maximum(
        jnp.max(top, axis=1, keepdims=True), jnp.max(own, axis=1, keepdims=True)
    )

    def add(r, carry):
        total, numer = carry
        p = jnp.exp2((sbuf[r] - row_max) * EXP_SCALE)
        total = total + (p[:, :HD] + p[:, HD:])
        numer = numer + jnp.dot(p.astype(jnp.bfloat16), vbuf[r], preferred_element_type=jnp.float32)
        return total, numer

    zero = jnp.zeros((ROWS, HD), jnp.float32)
    total, numer = lax.fori_loop(0, PAIRS, add, (zero, zero), unroll=4)
    p = jnp.exp2((own - row_max) * EXP_SCALE)
    numer = numer + jnp.dot(p.astype(jnp.bfloat16), own_values, preferred_element_type=jnp.float32)
    row_sum = jnp.sum(total, axis=1, keepdims=True) + jnp.sum(p, axis=1, keepdims=True)

    lane = lax.broadcasted_iota(jnp.int32, (SUF, HD), 1)
    maxima = jnp.zeros((SUF, HD), jnp.float32)
    sums = jnp.zeros((SUF, HD), jnp.float32)
    for g in range(GROUPS):
        part = slice(g * SUF, (g + 1) * SUF)
        smsg[pl.ds(g, SUF, stride=8), :] = numer[part]
        maxima = jnp.where(lane == g, row_max[part], maxima)
        sums = jnp.where(lane == g, row_sum[part], sums)
    smsg[pl.ds(6, SUF, stride=8), :] = maxima
    smsg[pl.ds(7, SUF, stride=8), :] = sums

    my_tile = pl.ds(pl.multiple_of(chip * 8, 8), 8)

    def send_state(step, carry):
        to = chip_at(step)
        pltpu.make_async_remote_copy(
            src_ref=smsg.at[pl.ds(pl.multiple_of(to * 8, 8), 8)], dst_ref=rbuf.at[my_tile],
            send_sem=send_sem.at[1], recv_sem=recv_sem.at[1],
            device_id=(to * 2 + core, tp), device_id_type=MESH,
        ).start()
        return carry

    lax.fori_loop(0, CHIPS - 1, send_state, 0)
    rbuf[my_tile, :] = smsg[my_tile, :]
    others = pl.ds(0, (CHIPS - 1) * 8)
    pltpu.make_async_copy(rbuf.at[others], rbuf.at[others], recv_sem.at[1]).wait()

    maxima = head_rows(rbuf, 6)
    sums = head_rows(rbuf, 7)
    best = jnp.max(maxima, axis=0, keepdims=True)
    scale = jnp.exp2((maxima - best) * EXP_SCALE)
    whole = jnp.sum(scale * sums, axis=0, keepdims=True)
    lane = lax.broadcasted_iota(jnp.int32, (1, HD), 1)
    scale = scale / jnp.where(lane < GROUPS, whole, 1.0)
    limit = jnp.where(core == 0, len_ref[:, 0:1], len_ref[:, 1:2])
    rows = []
    for g in range(GROUPS):
        row = jnp.sum(scale[:, g : g + 1] * head_rows(rbuf, g), axis=0, keepdims=True)
        rows.append(jnp.where(limit > chip, row, 0.0))
    rows.append(jnp.zeros((2, HD), jnp.float32))
    amsg[...] = jnp.concatenate(rows, axis=0)

    def send_attention(step, carry):
        to = chip_at(step)
        pltpu.make_async_remote_copy(
            src_ref=amsg, dst_ref=abuf.at[my_tile],
            send_sem=send_sem.at[2], recv_sem=recv_sem.at[2],
            device_id=(to * 2 + core, tp), device_id_type=MESH,
        ).start()
        return carry

    lax.fori_loop(0, CHIPS - 1, send_attention, 0)
    abuf[my_tile, :] = amsg[...]
    swaps[2].wait()
    pltpu.make_async_copy(abuf.at[others], abuf.at[others], recv_sem.at[2]).wait()

    attention = jnp.concatenate([head_rows(abuf, g) for g in range(GROUPS)], axis=1).astype(jnp.bfloat16)
    for side in range(2):
        share = jnp.dot(attention, wbuf[side], preferred_element_type=jnp.float32)
        for tile in range(TP // CONV):
            omsg[side, tile] = share[tile * 8 : (tile + 1) * 8]

    kept = core == lax.div(tp, TP // CONV)
    for side in range(2):
        for tile in range(TP // CONV):
            to = (chip * 2 + side, core * (TP // CONV) + tile)
            here = (to[0] == pool) & (to[1] == tp)

            @pl.when(jnp.logical_not(here))
            def _():
                pltpu.make_async_remote_copy(
                    src_ref=omsg.at[side, tile], dst_ref=obuf.at[tp],
                    send_sem=send_sem.at[3], recv_sem=recv_sem.at[3],
                    device_id=to, device_id_type=MESH,
                ).start()

            @pl.when(here)
            def _():
                pltpu.make_async_copy(omsg.at[side, tile], obuf.at[tp], recv_sem.at[3]).start()

    pltpu.make_async_copy(obuf, obuf, recv_sem.at[3]).wait()
    out_ref[...] = jnp.sum(obuf[...], axis=0).astype(out_ref.dtype)

    tiles = qbuf.at[others]
    for n in range(1, 3):
        pltpu.make_async_copy(tiles, tiles, send_sem.at[n]).wait()

    @pl.when(core == home)
    def _():
        pltpu.make_async_copy(tiles, tiles, send_sem.at[0]).wait()

    @pl.when(core != home)
    def _():
        pltpu.make_async_copy(qbuf, qbuf, send_sem.at[0]).wait()

    @pl.when(kept)
    def _():
        sent = obuf.at[pl.ds(0, TP - 1)]
        pltpu.make_async_copy(sent, sent, send_sem.at[3]).wait()

    @pl.when(jnp.logical_not(kept))
    def _():
        pltpu.make_async_copy(obuf, obuf, send_sem.at[3]).wait()


def shards(queries, suffix_keys, suffix_values, prefix_keys, prefix_values, block_slot, suffix_len, out_weight):
    f32, bf16 = jnp.float32, jnp.bfloat16
    columns = out_weight.shape[1]
    blocks = (PAIRS // 2, 2 * HD, HD)
    vmem = pl.BlockSpec(memory_space=pltpu.VMEM)
    anywhere = pl.BlockSpec(memory_space=pl.ANY)
    return pl.pallas_call(
        kernel,
        name="attend_and_project",
        out_shape=jax.ShapeDtypeStruct((8, columns), bf16),
        in_specs=[vmem, vmem, vmem, anywhere, anywhere, vmem, vmem, anywhere],
        out_specs=vmem,
        scratch_shapes=[
            pltpu.VMEM((8, HD), f32),
            pltpu.VMEM((SUF * 8, HD), f32),
            pltpu.VMEM((PAIRS, 2 * HD, HD), bf16),
            pltpu.VMEM((PAIRS, 2 * HD, HD), bf16),
            pltpu.VMEM((2, GROUPS * HD, columns), bf16),
            pltpu.VMEM((PAIRS, 2 * HD), f32),
            pltpu.VMEM((PAIRS, ROWS, 2 * HD), f32),
            pltpu.VMEM((SUF * 8, HD), f32),
            pltpu.VMEM((CHIPS * 8, HD), f32),
            pltpu.VMEM((8, HD), f32),
            pltpu.VMEM((CHIPS * 8, HD), f32),
            pltpu.VMEM((2, TP // CONV, 8, columns), f32),
            pltpu.VMEM((TP, 8, columns), f32),
            pltpu.SemaphoreType.DMA((3,)),
            pltpu.SemaphoreType.DMA((3,)),
            pltpu.SemaphoreType.DMA((3,)),
            pltpu.SemaphoreType.DMA((4,)),
            pltpu.SemaphoreType.DMA((4,)),
        ],
        compiler_params=pltpu.CompilerParams(
            collective_id=0, has_side_effects=True, vmem_limit_bytes=40 * 1024 * 1024
        ),
    )(
        queries,
        suffix_keys,
        suffix_values,
        prefix_keys.reshape(blocks),
        prefix_values.reshape(blocks),
        block_slot,
        suffix_len.reshape(1, CONV),
        out_weight,
    )


def solution(mesh):
    in_specs = (
        P("pool", "tp"),
        P("pool", "tp"),
        P("pool", "tp"),
        P("pool", None, "tp"),
        P("pool", None, "tp"),
        P(),
        P(),
        P("tp", "pool"),
    )
    return jax.shard_map(shards, mesh=mesh, in_specs=in_specs, out_specs=P("tp", "pool"), check_vma=False)
```

```python
import functools
import math

import jax
import jax.numpy as jnp
from jax import lax
from jax.experimental import pallas as pl
from jax.experimental.pallas import tpu as pltpu
from jax.sharding import PartitionSpec as P

H = 48
KVH = 8
HD = 128
CONV = 2
SUF = 32
GROUPS = H // KVH
NEG = -(2.0**100)
EXP_SCALE = math.log2(math.e) / math.sqrt(HD)
MESH = pl.DeviceIdType.MESH

NX = 4
NY = 8
CHIPS = NX * NY
TP = 8
PAIRS = 16
TILE = 8
TILES = SUF // TILE


def far_first(count, step):
    half = count // 2
    return half + (1 - 2 * (step % 2)) * ((step + 1) // 2)


NEARER = (
    (2, 1), (2, 7), (1, 2), (1, 6), (2, 0), (1, 1), (1, 7), (3, 1), (3, 7), (0, 2), (0, 6),
    (1, 0), (3, 0), (0, 1), (0, 7),
)


def opposite(chip):
    return (chip // NY + NX // 2) % NX * NY + (chip % NY + NY // 2) % NY


def couple(chip):
    across = chip // (CHIPS // 2)
    return chip - across * (CHIPS // 2) + across * ((chip % NY + NY // 2) % NY - chip % NY)


def kernel(
    q_hbm, sk_hbm, sv_hbm, keys_ref, values_ref, slot_hbm, len_hbm, w_ref,
    out_ref,
    q_ref, sk_ref, sv_ref, slot_ref, len_ref,
    qmsg, qbuf, kbuf, vbuf, wbuf, bias, sbuf, state, smsg, rbuf, merged, amsg, abuf, omsg, obuf,
    small_sem, local_sem, part_send, part_recv, query_sem, attend_sem, send_sem, recv_sem,
):
    pool = lax.axis_index("pool")
    tp = lax.axis_index("tp")
    core = lax.rem(pool, 2)
    chip = lax.div(pool, 2)
    x = lax.div(chip, NY)
    y = lax.rem(chip, NY)
    other = pool + 1 - 2 * core
    home = lax.div(x, NX // CONV)
    token = lax.rem(pool, SUF)

    row_of = [lax.rem(x + dx, NX) * NY for dx in range(NX)]
    place_of = [lax.rem(y + dy, NY) for dy in range(NY)]

    def chip_at(step):
        return row_of[far_first(NX, step % NX) % NX] + place_of[far_first(NY, step // NX) % NY]

    barrier = pltpu.get_barrier_semaphore()

    def greet(step, carry):
        to = chip_at(step)
        pl.semaphore_signal(barrier, inc=1, device_id=(to * 2 + core, tp), device_id_type=MESH)
        pl.semaphore_signal(barrier, inc=1, device_id=(to * 2 + 1 - core, tp), device_id_type=MESH)
        return carry

    for step in range(CHIPS - 1):
        greet(step, 0)

    def greet_tp(step, carry):
        to = lax.rem(tp + 1 + step, TP)
        pl.semaphore_signal(barrier, inc=1, device_id=(pool, to), device_id_type=MESH)
        pl.semaphore_signal(barrier, inc=1, device_id=(other, to), device_id_type=MESH)
        return carry

    for step in range(TP - 1):
        greet_tp(step, 0)
    pl.semaphore_signal(barrier, inc=1, device_id=(other, tp), device_id_type=MESH)

    small = [
        pltpu.make_async_copy(src, dst, small_sem.at[n])
        for n, (src, dst) in enumerate(
            [(q_hbm, q_ref), (sk_hbm, sk_ref), (sv_hbm, sv_ref), (slot_hbm, slot_ref), (len_hbm, len_ref)]
        )
    ]
    for copy in small:
        copy.start()
    local = [
        pltpu.make_async_copy(keys_ref, kbuf.at[pl.ds(0, PAIRS // 2)], local_sem.at[0]),
        pltpu.make_async_copy(values_ref, vbuf.at[pl.ds(0, PAIRS // 2)], local_sem.at[1]),
        pltpu.make_async_copy(w_ref, wbuf.at[core], local_sem.at[2]),
    ]
    for copy in local:
        copy.start()
    for copy in small:
        copy.wait()

    rows = [q_ref[:, g * HD : (g + 1) * HD].astype(jnp.float32) for g in range(GROUPS)]
    rows += [sk_ref[...].astype(jnp.float32), sv_ref[...].astype(jnp.float32)]
    qmsg[...] = jnp.concatenate(rows, axis=0)

    slots = jnp.where(core == 0, slot_ref[0:1, :], slot_ref[1:2, :])
    pair = lax.broadcasted_iota(jnp.int32, (PAIRS, 1), 0)
    first = jnp.where(pair < PAIRS // 2, pool * PAIRS, other * PAIRS - PAIRS) + 2 * pair
    for side in range(2):
        found = jnp.max(jnp.where(slots == first + side, 1.0, 0.0), axis=1, keepdims=True)
        bias[:, side * HD : (side + 1) * HD] = jnp.broadcast_to(
            jnp.where(found > 0.5, 0.0, NEG), (PAIRS, HD)
        )

    pl.semaphore_wait(barrier, 2 * (CHIPS - 1) + 2 * (TP - 1) + 1)

    for step in range(CHIPS):
        to = chip_at(step) * 2 + home
        mine = qbuf.at[pl.ds(pl.multiple_of(token * 8, 8), 8)]

        @pl.when(to != pool)
        def _():
            pltpu.make_async_remote_copy(
                src_ref=qmsg, dst_ref=mine, send_sem=send_sem.at[0], recv_sem=query_sem.at[token // TILE],
                device_id=(to, tp), device_id_type=MESH,
            ).start()

        @pl.when(to == pool)
        def _():
            pltpu.make_async_copy(qmsg, mine, query_sem.at[token // TILE]).start()

    swaps = [
        pltpu.make_async_remote_copy(
            src_ref=src, dst_ref=dst, send_sem=part_send.at[n], recv_sem=part_recv.at[n],
            device_id=(other, tp), device_id_type=MESH,
        )
        for n, (src, dst) in enumerate(
            [
                (keys_ref, kbuf.at[pl.ds(PAIRS // 2, PAIRS // 2)]),
                (values_ref, vbuf.at[pl.ds(PAIRS // 2, PAIRS // 2)]),
                (w_ref, wbuf.at[core]),
            ]
        )
    ]
    for copy in swaps:
        copy.start()
    for copy in local:
        copy.wait()
    swaps[0].wait()
    swaps[1].wait()

    contract = (((1,), (1,)), ((), ()))
    rows = GROUPS * TILE

    def wait_bytes(ref, sem):
        pltpu.make_async_copy(ref, ref, sem).wait()

    for tile in range(TILES):
        base = tile * TILE * 8
        here = pl.ds(base, TILE * 8)
        wait_bytes(qbuf.at[here], query_sem.at[tile])

        queries = jnp.concatenate(
            [qbuf[pl.ds(base + g, TILE, stride=8), :] for g in range(GROUPS)], axis=0
        ).astype(jnp.bfloat16)
        seen = TILE * (tile + 1)
        own_keys = qbuf[pl.ds(6, seen, stride=8), :].astype(jnp.bfloat16)
        own_values = qbuf[pl.ds(7, seen, stride=8), :].astype(jnp.bfloat16)
        top = jnp.full((rows, HD), NEG, jnp.float32)
        for r in range(PAIRS):
            s = lax.dot_general(queries, kbuf[r], contract, preferred_element_type=jnp.float32)
            s = s + bias[r : r + 1, :]
            sbuf[r] = s
            top = jnp.maximum(top, jnp.maximum(s[:, :HD], s[:, HD:]))
        own = lax.dot_general(queries, own_keys, contract, preferred_element_type=jnp.float32)
        row_pos = tile * TILE + lax.rem(lax.broadcasted_iota(jnp.int32, (rows, seen), 0), TILE)
        key_pos = lax.broadcasted_iota(jnp.int32, (rows, seen), 1)
        own = jnp.where((key_pos == chip) & (row_pos >= chip), own, NEG)
        row_max = jnp.maximum(
            jnp.max(top, axis=1, keepdims=True), jnp.max(own, axis=1, keepdims=True)
        )
        row_max = row_max.astype(jnp.bfloat16).astype(jnp.float32)

        p = jnp.exp2((own - row_max) * EXP_SCALE)
        row_sum = jnp.sum(p, axis=1, keepdims=True)
        numer = jnp.dot(p.astype(jnp.bfloat16), own_values, preferred_element_type=jnp.float32)
        total = jnp.zeros((rows, HD), jnp.float32)
        for r in range(PAIRS):
            p = jnp.exp2((sbuf[r] - row_max) * EXP_SCALE)
            total = total + (p[:, :HD] + p[:, HD:])
            numer = numer + jnp.dot(p.astype(jnp.bfloat16), vbuf[r], preferred_element_type=jnp.float32)
        row_sum = row_sum + jnp.sum(total, axis=1, keepdims=True)

        lane = lax.broadcasted_iota(jnp.int32, (TILE, HD), 1)
        rounded = row_sum.astype(jnp.bfloat16).astype(jnp.float32)
        left = row_sum - rounded
        maxima = jnp.zeros((TILE, HD), jnp.float32)
        sums = jnp.zeros((TILE, HD), jnp.float32)
        for g in range(GROUPS):
            part = slice(g * TILE, (g + 1) * TILE)
            state[pl.ds(base + g, TILE, stride=8), :] = numer[part]
            maxima = jnp.where(lane == g, row_max[part], maxima)
            sums = jnp.where(lane == g, rounded[part], sums)
            sums = jnp.where(lane == g + HD // 2, left[part], sums)
        state[pl.ds(base + 6, TILE, stride=8), :] = maxima
        state[pl.ds(base + 7, TILE, stride=8), :] = sums
        smsg[here, :] = state[here, :].astype(jnp.bfloat16)

        my_tile = rbuf.at[pl.ds(pl.multiple_of(chip * 16, 16), 16)]
        for u in range(tile * TILE // 2, (tile + 1) * TILE // 2):
            couple_rows = smsg.at[pl.ds(u * 16, 16)]
            for to in (u, opposite(u)):

                @pl.when(chip != to)
                def _():
                    pltpu.make_async_remote_copy(
                        src_ref=couple_rows, dst_ref=my_tile,
                        send_sem=send_sem.at[1], recv_sem=recv_sem.at[0],
                        device_id=(to * 2 + core, tp), device_id_type=MESH,
                    ).start()

                @pl.when(chip == to)
                def _():
                    pltpu.make_async_copy(couple_rows, my_tile, recv_sem.at[0]).start()

    wait_bytes(rbuf, recv_sem.at[0])
    merged[...] = rbuf[...].astype(jnp.float32)
    mine = couple(chip)
    lane = lax.broadcasted_iota(jnp.int32, (1, HD), 1)
    limit = jnp.where(core == 0, len_ref[:, 0:1], len_ref[:, 1:2])
    out_rows = []
    for half in range(2):

        def of_chips(row):
            return merged[pl.ds(half * 8 + row, CHIPS, stride=16), :]

        maxima = of_chips(6)
        sums = of_chips(7)
        sums = sums + pltpu.roll(sums, HD // 2, axis=1)
        best = jnp.max(maxima, axis=0, keepdims=True)
        scale = jnp.exp2((maxima - best) * EXP_SCALE)
        whole = jnp.sum(scale * sums, axis=0, keepdims=True)
        scale = scale / jnp.where(lane < GROUPS, whole, 1.0)
        for g in range(GROUPS):
            row = jnp.sum(scale[:, g : g + 1] * of_chips(g), axis=0, keepdims=True)
            out_rows.append(jnp.where(limit > 2 * mine + half, row, 0.0))
        out_rows.append(jnp.zeros((2, HD), jnp.float32))
    amsg[...] = jnp.concatenate(out_rows, axis=0).astype(jnp.bfloat16)

    my_couple = abuf.at[pl.ds(pl.multiple_of(mine * 16, 16), 16)]
    arrived = attend_sem.at[mine // (TILE // 2)]
    for dx, dy in NEARER:
        to = row_of[dx] + place_of[dy]
        pltpu.make_async_remote_copy(
            src_ref=amsg, dst_ref=my_couple, send_sem=send_sem.at[2], recv_sem=arrived,
            device_id=(to * 2 + core, tp), device_id_type=MESH,
        ).start()
    pltpu.make_async_copy(amsg, my_couple, arrived).start()
    swaps[2].wait()

    my_share = obuf.at[tp]
    for tile in range(TILES):
        here = pl.ds(tile * TILE * 8, TILE * 8)
        wait_bytes(abuf.at[here], attend_sem.at[tile])
        state[here, :] = abuf[here, :].astype(jnp.float32)
        attention = jnp.concatenate(
            [state[pl.ds(tile * TILE * 8 + g, TILE, stride=8), :] for g in range(GROUPS)], axis=1
        ).astype(jnp.bfloat16)
        for side in (1, 0):
            share = lax.dot_general(attention, wbuf[side], contract, preferred_element_type=jnp.float32)
            rest = jnp.concatenate(
                [share[:, HD:], jnp.zeros((TILE, 2 * HD - share.shape[1]), jnp.float32)], axis=1
            )
            omsg[side, tile] = jnp.concatenate([share[:, :HD], rest], axis=0).astype(jnp.bfloat16)
            to = (chip * 2 + side, core * TILES + tile)
            stays = (to[0] == pool) & (to[1] == tp)

            @pl.when(jnp.logical_not(stays))
            def _():
                pltpu.make_async_remote_copy(
                    src_ref=omsg.at[side, tile], dst_ref=my_share,
                    send_sem=send_sem.at[3], recv_sem=recv_sem.at[1],
                    device_id=to, device_id_type=MESH,
                ).start()

            @pl.when(stays)
            def _():
                pltpu.make_async_copy(omsg.at[side, tile], my_share, recv_sem.at[1]).start()

    wait_bytes(obuf, recv_sem.at[1])
    result = jnp.sum(obuf[...].astype(jnp.float32), axis=0)
    out_ref[:, :HD] = result[:TILE].astype(out_ref.dtype)
    out_ref[:, HD:] = result[TILE:, : out_ref.shape[1] - HD].astype(out_ref.dtype)

    wait_bytes(rbuf.at[pl.ds(0, (CHIPS - 1) * 16)], send_sem.at[1])
    wait_bytes(abuf.at[pl.ds(0, len(NEARER) * 16)], send_sem.at[2])

    @pl.when(core == home)
    def _():
        wait_bytes(qbuf.at[pl.ds(0, (CHIPS - 1) * 8)], send_sem.at[0])

    @pl.when(core != home)
    def _():
        wait_bytes(qbuf, send_sem.at[0])

    @pl.when(core == tp // TILES)
    def _():
        wait_bytes(obuf.at[pl.ds(0, TP - 1)], send_sem.at[3])

    @pl.when(core != tp // TILES)
    def _():
        wait_bytes(obuf, send_sem.at[3])


def shards(queries, suffix_keys, suffix_values, prefix_keys, prefix_values, block_slot, suffix_len, out_weight):
    f32, bf16 = jnp.float32, jnp.bfloat16
    columns = out_weight.shape[1]
    blocks = (PAIRS // 2, 2 * HD, HD)
    in_hbm = pl.BlockSpec(memory_space=pl.ANY)
    return pl.pallas_call(
        kernel,
        name="attend_and_project",
        out_shape=jax.ShapeDtypeStruct((8, columns), bf16),
        in_specs=[in_hbm] * 8,
        out_specs=pl.BlockSpec(memory_space=pltpu.VMEM),
        scratch_shapes=[
            pltpu.VMEM(queries.shape, bf16),
            pltpu.VMEM(suffix_keys.shape, bf16),
            pltpu.VMEM(suffix_values.shape, bf16),
            pltpu.VMEM(block_slot.shape, jnp.int32),
            pltpu.VMEM((1, CONV), jnp.int32),
            pltpu.VMEM((8, HD), f32),
            pltpu.VMEM((SUF * 8, HD), f32),
            pltpu.VMEM((PAIRS, 2 * HD, HD), bf16),
            pltpu.VMEM((PAIRS, 2 * HD, HD), bf16),
            pltpu.VMEM((2, columns, GROUPS * HD), bf16),
            pltpu.VMEM((PAIRS, 2 * HD), f32),
            pltpu.VMEM((PAIRS, GROUPS * TILE, 2 * HD), f32),
            pltpu.VMEM((SUF * 8, HD), f32),
            pltpu.VMEM((SUF * 8, HD), bf16),
            pltpu.VMEM((CHIPS * 16, HD), bf16),
            pltpu.VMEM((CHIPS * 16, HD), f32),
            pltpu.VMEM((16, HD), bf16),
            pltpu.VMEM((SUF * 8, HD), bf16),
            pltpu.VMEM((2, TILES, 2 * TILE, HD), bf16),
            pltpu.VMEM((TP, 2 * TILE, HD), bf16),
            pltpu.SemaphoreType.DMA((5,)),
            pltpu.SemaphoreType.DMA((3,)),
            pltpu.SemaphoreType.DMA((3,)),
            pltpu.SemaphoreType.DMA((3,)),
            pltpu.SemaphoreType.DMA((TILES,)),
            pltpu.SemaphoreType.DMA((TILES,)),
            pltpu.SemaphoreType.DMA((4,)),
            pltpu.SemaphoreType.DMA((2,)),
        ],
        compiler_params=pltpu.CompilerParams(
            collective_id=0, has_side_effects=True, vmem_limit_bytes=56 * 1024 * 1024
        ),
    )(
        queries,
        suffix_keys,
        suffix_values,
        prefix_keys.reshape(blocks),
        prefix_values.reshape(blocks),
        block_slot,
        suffix_len.reshape(1, CONV),
        out_weight.T,
    )


def solution(mesh):
    in_specs = (
        P("pool", "tp"),
        P("pool", "tp"),
        P("pool", "tp"),
        P("pool", None, "tp"),
        P("pool", None, "tp"),
        P(),
        P(),
        P("tp", "pool"),
    )
    return jax.shard_map(shards, mesh=mesh, in_specs=in_specs, out_specs=P("tp", "pool"), check_vma=False)
```

```python
import functools
import math

import jax
import jax.numpy as jnp
from jax import lax
from jax.experimental import pallas as pl
from jax.experimental.pallas import tpu as pltpu
from jax.sharding import PartitionSpec as P

H = 48
KVH = 8
HD = 128
CONV = 2
SUF = 32
GROUPS = H // KVH
NEG = -(2.0**100)
EXP_SCALE = math.log2(math.e) / math.sqrt(HD)
MESH = pl.DeviceIdType.MESH

NX = 4
NY = 8
CHIPS = NX * NY
TP = 8
PAIRS = 16
TILE = 8
TILES = SUF // TILE
GROUPED = ((0,), (1,), (2, 3))


def far_first(count, step):
    half = count // 2
    return half + (1 - 2 * (step % 2)) * ((step + 1) // 2)


CLASSES = 8
NEARER = ((2, 0), (1, 1), (1, 7), (1, 0), (3, 0), (0, 1), (0, 7))


def class_of(chip):
    return chip // NY % 2 * 4 + (chip % NY + 2 * (chip // (CHIPS // 2))) % 4


def owners(which):
    return [chip for chip in range(CHIPS) if class_of(chip) == which]


def kernel(
    q_hbm, sk_hbm, sv_hbm, keys_ref, values_ref, slot_hbm, len_hbm, w_ref,
    out_ref,
    q_ref, sk_ref, sv_ref, slot_ref, len_ref,
    qmsg, pmsg, qbuf, kbuf, vbuf, wbuf, bias, sbuf, state, smsg, rbuf, merged, amsg, abuf, omsg, obuf,
    small_sem, local_sem, part_send, part_recv, query_sem, attend_sem, send_sem, recv_sem, ready_sem,
):
    pool = lax.axis_index("pool")
    tp = lax.axis_index("tp")
    core = lax.rem(pool, 2)
    chip = lax.div(pool, 2)
    x = lax.div(chip, NY)
    y = lax.rem(chip, NY)
    other = pool + 1 - 2 * core
    home = lax.div(y, NY // 2)
    token = x * TILE + lax.rem(y, NY // 2) * 2 + core

    row_of = [lax.rem(x + dx, NX) * NY for dx in range(NX)]
    place_of = [lax.rem(y + dy, NY) for dy in range(NY)]

    def chip_at(step):
        return row_of[far_first(NX, step % NX) % NX] + place_of[far_first(NY, step // NX) % NY]

    barrier = pltpu.get_barrier_semaphore()

    def greet(step, carry):
        to = chip_at(step)
        pl.semaphore_signal(barrier, inc=1, device_id=(to * 2 + core, tp), device_id_type=MESH)
        pl.semaphore_signal(barrier, inc=1, device_id=(to * 2 + 1 - core, tp), device_id_type=MESH)
        return carry

    for step in range(CHIPS - 1):
        greet(step, 0)

    for step in range(1, TP):

        @pl.when(tp + step < TP)
        def _():
            for to in (pool, other):
                pl.semaphore_signal(barrier, inc=1, device_id=(to, tp + step), device_id_type=MESH)

    pl.semaphore_signal(barrier, inc=1, device_id=(other, tp), device_id_type=MESH)

    small = [
        pltpu.make_async_copy(src, dst, small_sem.at[n])
        for n, (src, dst) in enumerate(
            [(q_hbm, q_ref), (sk_hbm, sk_ref), (sv_hbm, sv_ref), (slot_hbm, slot_ref), (len_hbm, len_ref)]
        )
    ]
    for copy in small:
        copy.start()
    local = [
        pltpu.make_async_copy(keys_ref, kbuf.at[pl.ds(0, PAIRS // 2)], local_sem.at[0]),
        pltpu.make_async_copy(values_ref, vbuf.at[pl.ds(0, PAIRS // 2)], local_sem.at[1]),
        pltpu.make_async_copy(w_ref, wbuf.at[core], local_sem.at[2]),
    ]
    for copy in local:
        copy.start()
    for copy in small:
        copy.wait()

    rows = [q_ref[:, g * HD : (g + 1) * HD].astype(jnp.float32) for g in range(GROUPS)]
    rows += [sk_ref[...].astype(jnp.float32), sv_ref[...].astype(jnp.float32)]
    qmsg[...] = jnp.concatenate(rows, axis=0)

    pair = lax.broadcasted_iota(jnp.int32, (PAIRS, 1), 0)
    first = jnp.where(pair < PAIRS // 2, pool * PAIRS, other * PAIRS - PAIRS) + 2 * pair
    for conv in range(CONV):
        for side in range(2):
            found = jnp.max(
                jnp.where(slot_ref[conv : conv + 1, :] == first + side, 1.0, 0.0), axis=1, keepdims=True
            )
            bias[conv, :, side * HD : (side + 1) * HD] = jnp.broadcast_to(
                jnp.where(found > 0.5, 0.0, NEG), (PAIRS, HD)
            )

    pl.semaphore_wait(barrier, 2 * (CHIPS - 1) + 1 + 2 * tp)

    for step in range(CHIPS):
        to = chip_at(step) * 2 + home
        mine = qbuf.at[pl.ds(pl.multiple_of(token * 8, 8), 8)]

        @pl.when(to != pool)
        def _():
            pltpu.make_async_remote_copy(
                src_ref=qmsg, dst_ref=mine, send_sem=send_sem.at[0], recv_sem=query_sem.at[token // TILE],
                device_id=(to, tp), device_id_type=MESH,
            ).start()

        @pl.when(to == pool)
        def _():
            pltpu.make_async_copy(qmsg, mine, query_sem.at[token // TILE]).start()

    for step in range(1, TP):

        @pl.when(tp - step >= 0)
        def _():
            for to in (pool, other):
                pl.semaphore_signal(ready_sem, inc=1, device_id=(to, tp - step), device_id_type=MESH)

    swaps = [
        pltpu.make_async_remote_copy(
            src_ref=src, dst_ref=dst, send_sem=part_send.at[n], recv_sem=part_recv.at[n],
            device_id=(other, tp), device_id_type=MESH,
        )
        for n, (src, dst) in enumerate(
            [
                (keys_ref, kbuf.at[pl.ds(PAIRS // 2, PAIRS // 2)]),
                (values_ref, vbuf.at[pl.ds(PAIRS // 2, PAIRS // 2)]),
                (w_ref, wbuf.at[core]),
                (qmsg, pmsg),
            ]
        )
    ]
    for copy in swaps[3:] + swaps[:3]:
        copy.start()
    for copy in local:
        copy.wait()
    for n in (3, 0, 1):
        swaps[n].wait()

    contract = (((1,), (1,)), ((), ()))

    def wait_bytes(ref, sem):
        pltpu.make_async_copy(ref, ref, sem).wait()

    tiles = (qmsg[...], pmsg[...])
    tiles = (jnp.where(core == 0, tiles[0], tiles[1]), jnp.where(core == 0, tiles[1], tiles[0]))
    blank = jnp.zeros((6, HD), jnp.float32)
    own_keys, own_values = [
        jnp.concatenate([tiles[0][row : row + 1], tiles[1][row : row + 1], blank], axis=0).astype(jnp.bfloat16)
        for row in (6, 7)
    ]
    own_pos = lax.rem(x, 2) * (SUF // 2) + 2 * y

    for group in GROUPED:
        conv = group[0] // (TILES // CONV)
        tokens = TILE * len(group)
        rows = GROUPS * tokens
        base = group[0] * TILE * 8
        here = pl.ds(base, tokens * 8)
        for tile in group:
            wait_bytes(qbuf.at[pl.ds(tile * TILE * 8, TILE * 8)], query_sem.at[tile])

        queries = jnp.concatenate(
            [qbuf[pl.ds(base + g, tokens, stride=8), :] for g in range(GROUPS)], axis=0
        ).astype(jnp.bfloat16)
        top = jnp.full((rows, HD), NEG, jnp.float32)
        for r in range(PAIRS):
            s = lax.dot_general(queries, kbuf[r], contract, preferred_element_type=jnp.float32)
            s = s + bias[conv, r : r + 1, :]
            sbuf[r, 0:rows] = s
            top = jnp.maximum(top, jnp.maximum(s[:, :HD], s[:, HD:]))
        own = lax.dot_general(queries, own_keys, contract, preferred_element_type=jnp.float32)
        at = lax.rem(lax.broadcasted_iota(jnp.int32, (rows, 8), 0), tokens) + group[0] % 2 * TILE
        row_pos = (at // TILE * 2 + core) * TILE + at % TILE
        key = lax.broadcasted_iota(jnp.int32, (rows, 8), 1)
        own = jnp.where((key < 2) & (row_pos >= own_pos + key) & (x // 2 == conv), own, NEG)
        row_max = jnp.maximum(
            jnp.max(top, axis=1, keepdims=True), jnp.max(own, axis=1, keepdims=True)
        )
        row_max = row_max.astype(jnp.bfloat16).astype(jnp.float32)

        p = jnp.exp2((own - row_max) * EXP_SCALE)
        row_sum = jnp.sum(p, axis=1, keepdims=True)
        numer = jnp.dot(p.astype(jnp.bfloat16), own_values, preferred_element_type=jnp.float32)
        total = jnp.zeros((rows, HD), jnp.float32)
        for r in range(PAIRS):
            p = jnp.exp2((sbuf[r, 0:rows] - row_max) * EXP_SCALE)
            total = total + (p[:, :HD] + p[:, HD:])
            numer = numer + jnp.dot(p.astype(jnp.bfloat16), vbuf[r], preferred_element_type=jnp.float32)
        row_sum = row_sum + jnp.sum(total, axis=1, keepdims=True)

        lane = lax.broadcasted_iota(jnp.int32, (tokens, HD), 1)
        rounded = row_sum.astype(jnp.bfloat16).astype(jnp.float32)
        left = row_sum - rounded
        maxima = jnp.zeros((tokens, HD), jnp.float32)
        sums = jnp.zeros((tokens, HD), jnp.float32)
        for g in range(GROUPS):
            part = slice(g * tokens, (g + 1) * tokens)
            state[pl.ds(base + g, tokens, stride=8), :] = numer[part]
            maxima = jnp.where(lane == g, row_max[part], maxima)
            sums = jnp.where(lane == g, rounded[part], sums)
            sums = jnp.where(lane == g + HD // 2, left[part], sums)
        state[pl.ds(base + 6, tokens, stride=8), :] = maxima
        state[pl.ds(base + 7, tokens, stride=8), :] = sums
        smsg[here, :] = state[here, :].astype(jnp.bfloat16)

        my_tile = rbuf.at[conv, pl.ds(pl.multiple_of(chip * 16, 16), 16)]
        for couple in range(group[0] * TILE // 2, (group[-1] + 1) * TILE // 2):
            couple_rows = smsg.at[pl.ds(couple * 16, 16)]
            for to in owners(couple % CLASSES):

                @pl.when(chip != to)
                def _():
                    pltpu.make_async_remote_copy(
                        src_ref=couple_rows, dst_ref=my_tile,
                        send_sem=send_sem.at[1], recv_sem=recv_sem.at[conv],
                        device_id=(to * 2 + core, tp), device_id_type=MESH,
                    ).start()

                @pl.when(chip == to)
                def _():
                    pltpu.make_async_copy(couple_rows, my_tile, recv_sem.at[conv]).start()

    mine = class_of(chip)

    def merge(conv):
        wait_bytes(rbuf.at[conv], recv_sem.at[conv])
        merged[...] = rbuf[conv].astype(jnp.float32)
        lane = lax.broadcasted_iota(jnp.int32, (1, HD), 1)
        limit = len_ref[:, conv : conv + 1]
        out_rows = []
        for half in range(2):

            def of_chips(row):
                return merged[pl.ds(half * 8 + row, CHIPS, stride=16), :]

            maxima = of_chips(6)
            sums = of_chips(7)
            sums = sums + pltpu.roll(sums, HD // 2, axis=1)
            best = jnp.max(maxima, axis=0, keepdims=True)
            scale = jnp.exp2((maxima - best) * EXP_SCALE)
            whole = jnp.sum(scale * sums, axis=0, keepdims=True)
            scale = scale / jnp.where(lane < GROUPS, whole, 1.0)
            position = (mine // 4 * 2 + core) * TILE + mine % 4 * 2 + half
            for g in range(GROUPS):
                row = jnp.sum(scale[:, g : g + 1] * of_chips(g), axis=0, keepdims=True)
                out_rows.append(jnp.where(limit > position, row, 0.0))
            out_rows.append(jnp.zeros((2, HD), jnp.float32))
        amsg[conv] = jnp.concatenate(out_rows, axis=0).astype(jnp.bfloat16)

        my_couple = abuf.at[pl.ds(pl.multiple_of((conv * CLASSES + mine) * 16, 16), 16)]
        arrived = attend_sem.at[conv * 2 + mine // 4]
        for dx, dy in NEARER:
            to = row_of[dx] + place_of[dy]
            pltpu.make_async_remote_copy(
                src_ref=amsg.at[conv], dst_ref=my_couple, send_sem=send_sem.at[2], recv_sem=arrived,
                device_id=(to * 2 + core, tp), device_id_type=MESH,
            ).start()
        pltpu.make_async_copy(amsg.at[conv], my_couple, arrived).start()

    my_share = obuf.at[tp]

    def project(tile):
        here = pl.ds(tile * TILE * 8, TILE * 8)
        wait_bytes(abuf.at[here], attend_sem.at[tile])
        state[here, :] = abuf[here, :].astype(jnp.float32)
        attention = jnp.concatenate(
            [state[pl.ds(tile * TILE * 8 + g, TILE, stride=8), :] for g in range(GROUPS)], axis=1
        ).astype(jnp.bfloat16)
        for side in (1, 0):
            share = lax.dot_general(attention, wbuf[side], contract, preferred_element_type=jnp.float32)
            rest = jnp.concatenate(
                [share[:, HD:], jnp.zeros((TILE, 2 * HD - share.shape[1]), jnp.float32)], axis=1
            )
            omsg[side, tile] = jnp.concatenate([share[:, :HD], rest], axis=0).astype(jnp.bfloat16)
            to = (chip * 2 + side, 2 * tile + core)
            stays = (to[0] == pool) & (to[1] == tp)

            @pl.when(jnp.logical_not(stays))
            def _():
                pltpu.make_async_remote_copy(
                    src_ref=omsg.at[side, tile], dst_ref=my_share,
                    send_sem=send_sem.at[3], recv_sem=recv_sem.at[2],
                    device_id=to, device_id_type=MESH,
                ).start()

            @pl.when(stays)
            def _():
                pltpu.make_async_copy(omsg.at[side, tile], my_share, recv_sem.at[2]).start()

    merge(0)
    swaps[2].wait()

    @pl.when(tp < TP - 1)
    def _():
        pl.semaphore_wait(ready_sem, 2 * (TP - 1 - tp))

    project(0)
    project(1)
    merge(1)
    project(2)
    project(3)

    wait_bytes(obuf, recv_sem.at[2])
    result = jnp.sum(obuf[...].astype(jnp.float32), axis=0)
    out_ref[:, :HD] = result[:TILE].astype(out_ref.dtype)
    out_ref[:, HD:] = result[TILE:, : out_ref.shape[1] - HD].astype(out_ref.dtype)

    for conv in range(CONV):
        wait_bytes(rbuf.at[conv, pl.ds(0, (CHIPS - 1) * 16)], send_sem.at[1])
        wait_bytes(abuf.at[pl.ds(0, len(NEARER) * 16)], send_sem.at[2])

    @pl.when(core == home)
    def _():
        wait_bytes(qbuf.at[pl.ds(0, (CHIPS - 1) * 8)], send_sem.at[0])

    @pl.when(core != home)
    def _():
        wait_bytes(qbuf, send_sem.at[0])

    @pl.when(core == tp % 2)
    def _():
        wait_bytes(obuf.at[pl.ds(0, TP - 1)], send_sem.at[3])

    @pl.when(core != tp % 2)
    def _():
        wait_bytes(obuf, send_sem.at[3])


def shards(queries, suffix_keys, suffix_values, prefix_keys, prefix_values, block_slot, suffix_len, out_weight):
    f32, bf16 = jnp.float32, jnp.bfloat16
    columns = out_weight.shape[1]
    blocks = (PAIRS // 2, 2 * HD, HD)
    in_hbm = pl.BlockSpec(memory_space=pl.ANY)
    return pl.pallas_call(
        kernel,
        name="attend_and_project",
        out_shape=jax.ShapeDtypeStruct((8, columns), bf16),
        in_specs=[in_hbm] * 8,
        out_specs=pl.BlockSpec(memory_space=pltpu.VMEM),
        scratch_shapes=[
            pltpu.VMEM(queries.shape, bf16),
            pltpu.VMEM(suffix_keys.shape, bf16),
            pltpu.VMEM(suffix_values.shape, bf16),
            pltpu.VMEM(block_slot.shape, jnp.int32),
            pltpu.VMEM((1, CONV), jnp.int32),
            pltpu.VMEM((8, HD), f32),
            pltpu.VMEM((8, HD), f32),
            pltpu.VMEM((SUF * 8, HD), f32),
            pltpu.VMEM((PAIRS, 2 * HD, HD), bf16),
            pltpu.VMEM((PAIRS, 2 * HD, HD), bf16),
            pltpu.VMEM((2, columns, GROUPS * HD), bf16),
            pltpu.VMEM((CONV, PAIRS, 2 * HD), f32),
            pltpu.VMEM((PAIRS, GROUPS * TILE * max(map(len, GROUPED)), 2 * HD), f32),
            pltpu.VMEM((SUF * 8, HD), f32),
            pltpu.VMEM((SUF * 8, HD), bf16),
            pltpu.VMEM((CONV, CHIPS * 16, HD), bf16),
            pltpu.VMEM((CHIPS * 16, HD), f32),
            pltpu.VMEM((CONV, 16, HD), bf16),
            pltpu.VMEM((SUF * 8, HD), bf16),
            pltpu.VMEM((2, TILES, 2 * TILE, HD), bf16),
            pltpu.VMEM((TP, 2 * TILE, HD), bf16),
            pltpu.SemaphoreType.DMA((5,)),
            pltpu.SemaphoreType.DMA((3,)),
            pltpu.SemaphoreType.DMA((4,)),
            pltpu.SemaphoreType.DMA((4,)),
            pltpu.SemaphoreType.DMA((TILES,)),
            pltpu.SemaphoreType.DMA((TILES,)),
            pltpu.SemaphoreType.DMA((4,)),
            pltpu.SemaphoreType.DMA((3,)),
            pltpu.SemaphoreType.REGULAR,
        ],
        compiler_params=pltpu.CompilerParams(
            collective_id=0, has_side_effects=True, vmem_limit_bytes=56 * 1024 * 1024
        ),
    )(
        queries,
        suffix_keys,
        suffix_values,
        prefix_keys.reshape(blocks),
        prefix_values.reshape(blocks),
        block_slot,
        suffix_len.reshape(1, CONV),
        out_weight.T,
    )


def solution(mesh):
    in_specs = (
        P("pool", "tp"),
        P("pool", "tp"),
        P("pool", "tp"),
        P("pool", None, "tp"),
        P("pool", None, "tp"),
        P(),
        P(),
        P("tp", "pool"),
    )
    return jax.shard_map(shards, mesh=mesh, in_specs=in_specs, out_specs=P("tp", "pool"), check_vma=False)
```

```python
import functools
import math

import jax
import jax.numpy as jnp
from jax import lax
from jax.experimental import pallas as pl
from jax.experimental.pallas import tpu as pltpu
from jax.sharding import PartitionSpec as P

H = 48
KVH = 8
HD = 128
CONV = 2
SUF = 32
GROUPS = H // KVH
NEG = -(2.0**100)
EXP_SCALE = math.log2(math.e) / math.sqrt(HD)
MESH = pl.DeviceIdType.MESH

NX = 4
NY = 8
CHIPS = NX * NY
TP = 8
PAIRS = 16
TILE = 8
TILES = SUF // TILE
GROUPED = ((0,), (1,), (2, 3))


def far_first(count, step):
    half = count // 2
    return half + (1 - 2 * (step % 2)) * ((step + 1) // 2)


CLASSES = 8
NEARER = ((2, 0), (1, 1), (1, 7), (1, 0), (3, 0), (0, 1), (0, 7))


def class_of(chip):
    return chip // NY % 2 * 4 + (chip % NY + 2 * (chip // (CHIPS // 2))) % 4


def owners(which):
    return [chip for chip in range(CHIPS) if class_of(chip) == which]


LAST_X, LAST_Y = 2, 4


def hops_to_last(chip):
    return abs(chip // NY - LAST_X) + abs(chip % NY - LAST_Y)


def kernel(
    q_hbm, sk_hbm, sv_hbm, keys_ref, values_ref, slot_hbm, len_hbm, w_ref,
    out_ref,
    q_ref, sk_ref, sv_ref, slot_ref, len_ref,
    qmsg, pmsg, qbuf, kbuf, vbuf, wbuf, bias, sbuf, state, smsg, rbuf, merged, amsg, abuf, omsg, obuf,
    small_sem, local_sem, part_send, part_recv, query_sem, attend_sem, send_sem, recv_sem, ready_sem,
):
    pool = lax.axis_index("pool")
    tp = lax.axis_index("tp")
    core = lax.rem(pool, 2)
    chip = lax.div(pool, 2)
    x = lax.div(chip, NY)
    y = lax.rem(chip, NY)
    other = pool + 1 - 2 * core
    home = lax.div(y, NY // 2)
    token = x * TILE + lax.rem(y, NY // 2) * 2 + core

    row_of = [lax.rem(x + dx, NX) * NY for dx in range(NX)]
    place_of = [lax.rem(y + dy, NY) for dy in range(NY)]

    def chip_at(step):
        return row_of[far_first(NX, step % NX) % NX] + place_of[far_first(NY, step // NX) % NY]

    barrier = pltpu.get_barrier_semaphore()

    def greet(step, carry):
        to = chip_at(step)
        pl.semaphore_signal(barrier, inc=1, device_id=(to * 2 + core, tp), device_id_type=MESH)
        pl.semaphore_signal(barrier, inc=1, device_id=(to * 2 + 1 - core, tp), device_id_type=MESH)
        return carry

    for step in range(CHIPS - 1):
        greet(step, 0)

    for step in range(1, TP):

        @pl.when(tp + step < TP)
        def _():
            for to in (pool, other):
                pl.semaphore_signal(barrier, inc=1, device_id=(to, tp + step), device_id_type=MESH)

    pl.semaphore_signal(barrier, inc=1, device_id=(other, tp), device_id_type=MESH)

    small = [
        pltpu.make_async_copy(src, dst, small_sem.at[n])
        for n, (src, dst) in enumerate(
            [(q_hbm, q_ref), (sk_hbm, sk_ref), (sv_hbm, sv_ref), (slot_hbm, slot_ref), (len_hbm, len_ref)]
        )
    ]
    for copy in small:
        copy.start()
    local = [
        pltpu.make_async_copy(keys_ref, kbuf.at[pl.ds(0, PAIRS // 2)], local_sem.at[0]),
        pltpu.make_async_copy(values_ref, vbuf.at[pl.ds(0, PAIRS // 2)], local_sem.at[1]),
        pltpu.make_async_copy(w_ref, wbuf.at[core], local_sem.at[2]),
    ]
    for copy in local:
        copy.start()
    for copy in small:
        copy.wait()

    rows = [q_ref[:, g * HD : (g + 1) * HD].astype(jnp.float32) for g in range(GROUPS)]
    rows += [sk_ref[...].astype(jnp.float32), sv_ref[...].astype(jnp.float32)]
    qmsg[...] = jnp.concatenate(rows, axis=0).astype(jnp.bfloat16)

    pair = lax.broadcasted_iota(jnp.int32, (PAIRS, 1), 0)
    first = jnp.where(pair < PAIRS // 2, pool * PAIRS, other * PAIRS - PAIRS) + 2 * pair
    for conv in range(CONV):
        for side in range(2):
            found = jnp.max(
                jnp.where(slot_ref[conv : conv + 1, :] == first + side, 1.0, 0.0), axis=1, keepdims=True
            )
            bias[conv, :, side * HD : (side + 1) * HD] = jnp.broadcast_to(
                jnp.where(found > 0.5, 0.0, NEG), (PAIRS, HD)
            )

    pl.semaphore_wait(barrier, 2 * (CHIPS - 1) + 1 + 2 * tp)

    for step in range(CHIPS):
        to = chip_at(step) * 2 + home
        mine = qbuf.at[token]

        @pl.when(to != pool)
        def _():
            pltpu.make_async_remote_copy(
                src_ref=qmsg, dst_ref=mine, send_sem=send_sem.at[0], recv_sem=query_sem.at[token // TILE],
                device_id=(to, tp), device_id_type=MESH,
            ).start()

        @pl.when(to == pool)
        def _():
            pltpu.make_async_copy(qmsg, mine, query_sem.at[token // TILE]).start()

    for step in range(1, TP):

        @pl.when(tp - step >= 0)
        def _():
            for to in (pool, other):
                pl.semaphore_signal(ready_sem, inc=1, device_id=(to, tp - step), device_id_type=MESH)

    swaps = [
        pltpu.make_async_remote_copy(
            src_ref=src, dst_ref=dst, send_sem=part_send.at[n], recv_sem=part_recv.at[n],
            device_id=(other, tp), device_id_type=MESH,
        )
        for n, (src, dst) in enumerate(
            [
                (keys_ref, kbuf.at[pl.ds(PAIRS // 2, PAIRS // 2)]),
                (values_ref, vbuf.at[pl.ds(PAIRS // 2, PAIRS // 2)]),
                (w_ref, wbuf.at[core]),
                (qmsg, pmsg),
            ]
        )
    ]
    for copy in swaps[3:] + swaps[:3]:
        copy.start()
    for copy in local:
        copy.wait()
    for n in (3, 0, 1):
        swaps[n].wait()

    contract = (((1,), (1,)), ((), ()))

    def wait_bytes(ref, sem):
        pltpu.make_async_copy(ref, ref, sem).wait()

    tiles = (qmsg[...].astype(jnp.float32), pmsg[...].astype(jnp.float32))
    tiles = (jnp.where(core == 0, tiles[0], tiles[1]), jnp.where(core == 0, tiles[1], tiles[0]))
    blank = jnp.zeros((6, HD), jnp.float32)
    own_keys, own_values = [
        jnp.concatenate([tiles[0][row : row + 1], tiles[1][row : row + 1], blank], axis=0).astype(jnp.bfloat16)
        for row in (6, 7)
    ]
    own_pos = lax.rem(x, 2) * (SUF // 2) + 2 * y

    for group in GROUPED:
        conv = group[0] // (TILES // CONV)
        tokens = TILE * len(group)
        rows = GROUPS * tokens
        base = group[0] * TILE * 8
        here = pl.ds(base, tokens * 8)
        for tile in group:
            wait_bytes(qbuf.at[pl.ds(tile * TILE, TILE)], query_sem.at[tile])

        state[here, :] = qbuf[group[0] * TILE : group[0] * TILE + tokens].astype(jnp.float32).reshape(tokens * 8, HD)
        queries = jnp.concatenate(
            [state[pl.ds(base + g, tokens, stride=8), :] for g in range(GROUPS)], axis=0
        ).astype(jnp.bfloat16)
        top = jnp.full((rows, HD), NEG, jnp.float32)
        for r in range(PAIRS):
            s = lax.dot_general(queries, kbuf[r], contract, preferred_element_type=jnp.float32)
            s = s + bias[conv, r : r + 1, :]
            sbuf[r, 0:rows] = s
            top = jnp.maximum(top, jnp.maximum(s[:, :HD], s[:, HD:]))
        own = lax.dot_general(queries, own_keys, contract, preferred_element_type=jnp.float32)
        at = lax.rem(lax.broadcasted_iota(jnp.int32, (rows, 8), 0), tokens) + group[0] % 2 * TILE
        row_pos = (at // TILE * 2 + core) * TILE + at % TILE
        key = lax.broadcasted_iota(jnp.int32, (rows, 8), 1)
        own = jnp.where((key < 2) & (row_pos >= own_pos + key) & (x // 2 == conv), own, NEG)
        row_max = jnp.maximum(
            jnp.max(top, axis=1, keepdims=True), jnp.max(own, axis=1, keepdims=True)
        )
        row_max = row_max.astype(jnp.bfloat16).astype(jnp.float32)

        p = jnp.exp2((own - row_max) * EXP_SCALE)
        row_sum = jnp.sum(p, axis=1, keepdims=True)
        numer = jnp.dot(p.astype(jnp.bfloat16), own_values, preferred_element_type=jnp.float32)
        total = jnp.zeros((rows, HD), jnp.float32)
        for r in range(PAIRS):
            p = jnp.exp2((sbuf[r, 0:rows] - row_max) * EXP_SCALE)
            total = total + (p[:, :HD] + p[:, HD:])
            numer = numer + jnp.dot(p.astype(jnp.bfloat16), vbuf[r], preferred_element_type=jnp.float32)
        row_sum = row_sum + jnp.sum(total, axis=1, keepdims=True)

        lane = lax.broadcasted_iota(jnp.int32, (tokens, HD), 1)
        rounded = row_sum.astype(jnp.bfloat16).astype(jnp.float32)
        left = row_sum - rounded
        maxima = jnp.zeros((tokens, HD), jnp.float32)
        sums = jnp.zeros((tokens, HD), jnp.float32)
        for g in range(GROUPS):
            part = slice(g * tokens, (g + 1) * tokens)
            state[pl.ds(base + g, tokens, stride=8), :] = numer[part]
            maxima = jnp.where(lane == g, row_max[part], maxima)
            sums = jnp.where(lane == g, rounded[part], sums)
            sums = jnp.where(lane == g + HD // 2, left[part], sums)
        state[pl.ds(base + 6, tokens, stride=8), :] = maxima
        state[pl.ds(base + 7, tokens, stride=8), :] = sums
        smsg[here, :] = state[here, :].astype(jnp.bfloat16)

        my_tile = rbuf.at[conv, pl.ds(pl.multiple_of(chip * 16, 16), 16)]
        targets = [
            (to, couple)
            for couple in range(group[0] * TILE // 2, (group[-1] + 1) * TILE // 2)
            for to in owners(couple % CLASSES)
        ]
        for to, couple in sorted(targets, key=lambda target: -hops_to_last(target[0])):
            couple_rows = smsg.at[pl.ds(couple * 16, 16)]

            @pl.when(chip != to)
            def _():
                pltpu.make_async_remote_copy(
                    src_ref=couple_rows, dst_ref=my_tile,
                    send_sem=send_sem.at[1], recv_sem=recv_sem.at[conv],
                    device_id=(to * 2 + core, tp), device_id_type=MESH,
                ).start()

            @pl.when(chip == to)
            def _():
                pltpu.make_async_copy(couple_rows, my_tile, recv_sem.at[conv]).start()

    mine = class_of(chip)

    def merge(conv):
        wait_bytes(rbuf.at[conv], recv_sem.at[conv])
        merged[...] = rbuf[conv].astype(jnp.float32)
        lane = lax.broadcasted_iota(jnp.int32, (1, HD), 1)
        limit = len_ref[:, conv : conv + 1]
        out_rows = []
        for half in range(2):

            def of_chips(row):
                return merged[pl.ds(half * 8 + row, CHIPS, stride=16), :]

            maxima = of_chips(6)
            sums = of_chips(7)
            sums = sums + pltpu.roll(sums, HD // 2, axis=1)
            best = jnp.max(maxima, axis=0, keepdims=True)
            scale = jnp.exp2((maxima - best) * EXP_SCALE)
            whole = jnp.sum(scale * sums, axis=0, keepdims=True)
            scale = scale / jnp.where(lane < GROUPS, whole, 1.0)
            position = (mine // 4 * 2 + core) * TILE + mine % 4 * 2 + half
            for g in range(GROUPS):
                row = jnp.sum(scale[:, g : g + 1] * of_chips(g), axis=0, keepdims=True)
                out_rows.append(jnp.where(limit > position, row, 0.0))
            out_rows.append(jnp.zeros((2, HD), jnp.float32))
        amsg[conv] = jnp.concatenate(out_rows, axis=0).astype(jnp.bfloat16)

        my_couple = abuf.at[pl.ds(pl.multiple_of((conv * CLASSES + mine) * 16, 16), 16)]
        arrived = attend_sem.at[conv * 2 + mine // 4]
        for dx, dy in NEARER:
            to = row_of[dx] + place_of[dy]
            pltpu.make_async_remote_copy(
                src_ref=amsg.at[conv], dst_ref=my_couple, send_sem=send_sem.at[2], recv_sem=arrived,
                device_id=(to * 2 + core, tp), device_id_type=MESH,
            ).start()
        pltpu.make_async_copy(amsg.at[conv], my_couple, arrived).start()

    my_share = obuf.at[tp]

    def project(tile):
        here = pl.ds(tile * TILE * 8, TILE * 8)
        wait_bytes(abuf.at[here], attend_sem.at[tile])
        state[here, :] = abuf[here, :].astype(jnp.float32)
        attention = jnp.concatenate(
            [state[pl.ds(tile * TILE * 8 + g, TILE, stride=8), :] for g in range(GROUPS)], axis=1
        ).astype(jnp.bfloat16)
        for side in (1, 0):
            share = lax.dot_general(attention, wbuf[side], contract, preferred_element_type=jnp.float32)
            rest = jnp.concatenate(
                [share[:, HD:], jnp.zeros((TILE, 2 * HD - share.shape[1]), jnp.float32)], axis=1
            )
            omsg[side, tile] = jnp.concatenate([share[:, :HD], rest], axis=0).astype(jnp.bfloat16)
            to = (chip * 2 + side, 2 * tile + core)
            stays = (to[0] == pool) & (to[1] == tp)

            @pl.when(jnp.logical_not(stays))
            def _():
                pltpu.make_async_remote_copy(
                    src_ref=omsg.at[side, tile], dst_ref=my_share,
                    send_sem=send_sem.at[3], recv_sem=recv_sem.at[2],
                    device_id=to, device_id_type=MESH,
                ).start()

            @pl.when(stays)
            def _():
                pltpu.make_async_copy(omsg.at[side, tile], my_share, recv_sem.at[2]).start()

    merge(0)
    swaps[2].wait()

    @pl.when(tp < TP - 1)
    def _():
        pl.semaphore_wait(ready_sem, 2 * (TP - 1 - tp))

    project(0)
    merge(1)
    project(1)
    project(2)
    project(3)

    wait_bytes(obuf, recv_sem.at[2])
    result = jnp.sum(obuf[...].astype(jnp.float32), axis=0)
    out_ref[:, :HD] = result[:TILE].astype(out_ref.dtype)
    out_ref[:, HD:] = result[TILE:, : out_ref.shape[1] - HD].astype(out_ref.dtype)

    for conv in range(CONV):
        wait_bytes(rbuf.at[conv, pl.ds(0, (CHIPS - 1) * 16)], send_sem.at[1])
        wait_bytes(abuf.at[pl.ds(0, len(NEARER) * 16)], send_sem.at[2])

    @pl.when(core == home)
    def _():
        wait_bytes(qbuf.at[pl.ds(0, CHIPS - 1)], send_sem.at[0])

    @pl.when(core != home)
    def _():
        wait_bytes(qbuf, send_sem.at[0])

    @pl.when(core == tp % 2)
    def _():
        wait_bytes(obuf.at[pl.ds(0, TP - 1)], send_sem.at[3])

    @pl.when(core != tp % 2)
    def _():
        wait_bytes(obuf, send_sem.at[3])


def shards(queries, suffix_keys, suffix_values, prefix_keys, prefix_values, block_slot, suffix_len, out_weight):
    f32, bf16 = jnp.float32, jnp.bfloat16
    columns = out_weight.shape[1]
    blocks = (PAIRS // 2, 2 * HD, HD)
    in_hbm = pl.BlockSpec(memory_space=pl.ANY)
    return pl.pallas_call(
        kernel,
        name="attend_and_project",
        out_shape=jax.ShapeDtypeStruct((8, columns), bf16),
        in_specs=[in_hbm] * 8,
        out_specs=pl.BlockSpec(memory_space=pltpu.VMEM),
        scratch_shapes=[
            pltpu.VMEM(queries.shape, bf16),
            pltpu.VMEM(suffix_keys.shape, bf16),
            pltpu.VMEM(suffix_values.shape, bf16),
            pltpu.VMEM(block_slot.shape, jnp.int32),
            pltpu.VMEM((1, CONV), jnp.int32),
            pltpu.VMEM((8, HD), bf16),
            pltpu.VMEM((8, HD), bf16),
            pltpu.VMEM((SUF, 8, HD), bf16),
            pltpu.VMEM((PAIRS, 2 * HD, HD), bf16),
            pltpu.VMEM((PAIRS, 2 * HD, HD), bf16),
            pltpu.VMEM((2, columns, GROUPS * HD), bf16),
            pltpu.VMEM((CONV, PAIRS, 2 * HD), f32),
            pltpu.VMEM((PAIRS, GROUPS * TILE * max(map(len, GROUPED)), 2 * HD), f32),
            pltpu.VMEM((SUF * 8, HD), f32),
            pltpu.VMEM((SUF * 8, HD), bf16),
            pltpu.VMEM((CONV, CHIPS * 16, HD), bf16),
            pltpu.VMEM((CHIPS * 16, HD), f32),
            pltpu.VMEM((CONV, 16, HD), bf16),
            pltpu.VMEM((SUF * 8, HD), bf16),
            pltpu.VMEM((2, TILES, 2 * TILE, HD), bf16),
            pltpu.VMEM((TP, 2 * TILE, HD), bf16),
            pltpu.SemaphoreType.DMA((5,)),
            pltpu.SemaphoreType.DMA((3,)),
            pltpu.SemaphoreType.DMA((4,)),
            pltpu.SemaphoreType.DMA((4,)),
            pltpu.SemaphoreType.DMA((TILES,)),
            pltpu.SemaphoreType.DMA((TILES,)),
            pltpu.SemaphoreType.DMA((4,)),
            pltpu.SemaphoreType.DMA((3,)),
            pltpu.SemaphoreType.REGULAR,
        ],
        compiler_params=pltpu.CompilerParams(
            collective_id=0, has_side_effects=True, vmem_limit_bytes=55040 * 1024
        ),
    )(
        queries,
        suffix_keys,
        suffix_values,
        prefix_keys.reshape(blocks),
        prefix_values.reshape(blocks),
        block_slot,
        suffix_len.reshape(1, CONV),
        out_weight.T,
    )


def solution(mesh):
    in_specs = (
        P("pool", "tp"),
        P("pool", "tp"),
        P("pool", "tp"),
        P("pool", None, "tp"),
        P("pool", None, "tp"),
        P(),
        P(),
        P("tp", "pool"),
    )
    return jax.shard_map(shards, mesh=mesh, in_specs=in_specs, out_specs=P("tp", "pool"), check_vma=False)
```

```python
import functools
import math

import jax
import jax.numpy as jnp
from jax import lax
from jax.experimental import pallas as pl
from jax.experimental.pallas import tpu as pltpu
from jax.sharding import PartitionSpec as P

H = 48
KVH = 8
HD = 128
CONV = 2
SUF = 32
GROUPS = H // KVH
NEG = -(2.0**100)
EXP_SCALE = math.log2(math.e) / math.sqrt(HD)
MESH = pl.DeviceIdType.MESH

NX = 4
NY = 8
CHIPS = NX * NY
TP = 8
PAIRS = 16
TILE = 8
TILES = SUF // TILE
GROUPED = ((0,), (1,), (2, 3))


def far_first(count, step):
    half = count // 2
    return half + (1 - 2 * (step % 2)) * ((step + 1) // 2)


CLASSES = 8
NEARER = (
    ((2, 0), (1, 1), (1, 7), (1, 0), (3, 0), (0, 1), (0, 7)),
    (
        (2, 2), (3, 2), (1, 2), (2, 7), (2, 1), (0, 2), (3, 7), (3, 1),
        (2, 0), (1, 1), (1, 7), (1, 0), (3, 0), (0, 1), (0, 7),
    ),
)


def class_of(chip):
    return chip // NY % 2 * 4 + (chip % NY + 2 * (chip // (CHIPS // 2))) % 4


def owners(which, conv):
    return [chip for chip in range(CHIPS // (1 + conv)) if class_of(chip) == which]


LAST_X, LAST_Y = 2, 4


def hops_to_last(chip):
    return abs(chip // NY - LAST_X) + abs(chip % NY - LAST_Y)


def kernel(
    q_hbm, sk_hbm, sv_hbm, keys_ref, values_ref, slot_hbm, len_hbm, w_ref,
    out_ref,
    q_ref, sk_ref, sv_ref, slot_ref, len_ref,
    qmsg, pmsg, qbuf, kbuf, vbuf, wbuf, bias, sbuf, state, smsg, rbuf, fbuf, merged, amsg, abuf, omsg, obuf,
    small_sem, local_sem, part_send, part_recv, query_sem, attend_sem, send_sem, recv_sem, first_sem, ready_sem,
):
    pool = lax.axis_index("pool")
    tp = lax.axis_index("tp")
    core = lax.rem(pool, 2)
    chip = lax.div(pool, 2)
    x = lax.div(chip, NY)
    y = lax.rem(chip, NY)
    other = pool + 1 - 2 * core
    home = lax.div(y, NY // 2)
    token = x * TILE + lax.rem(y, NY // 2) * 2 + core

    row_of = [lax.rem(x + dx, NX) * NY for dx in range(NX)]
    place_of = [lax.rem(y + dy, NY) for dy in range(NY)]

    def chip_at(step):
        return row_of[far_first(NX, step % NX) % NX] + place_of[far_first(NY, step // NX) % NY]

    barrier = pltpu.get_barrier_semaphore()

    def greet(step, carry):
        to = chip_at(step)
        pl.semaphore_signal(barrier, inc=1, device_id=(to * 2 + core, tp), device_id_type=MESH)
        pl.semaphore_signal(barrier, inc=1, device_id=(to * 2 + 1 - core, tp), device_id_type=MESH)
        return carry

    for step in range(CHIPS - 1):
        greet(step, 0)

    for step in range(1, TP):

        @pl.when(tp + step < TP)
        def _():
            for to in (pool, other):
                pl.semaphore_signal(barrier, inc=1, device_id=(to, tp + step), device_id_type=MESH)

    pl.semaphore_signal(barrier, inc=1, device_id=(other, tp), device_id_type=MESH)

    small = [
        pltpu.make_async_copy(src, dst, small_sem.at[n])
        for n, (src, dst) in enumerate(
            [(q_hbm, q_ref), (sk_hbm, sk_ref), (sv_hbm, sv_ref), (slot_hbm, slot_ref), (len_hbm, len_ref)]
        )
    ]
    for copy in small:
        copy.start()
    local = [
        pltpu.make_async_copy(keys_ref, kbuf.at[pl.ds(0, PAIRS // 2)], local_sem.at[0]),
        pltpu.make_async_copy(values_ref, vbuf.at[pl.ds(0, PAIRS // 2)], local_sem.at[1]),
        pltpu.make_async_copy(w_ref, wbuf.at[core], local_sem.at[2]),
    ]
    for copy in local:
        copy.start()
    for copy in small:
        copy.wait()

    rows = [q_ref[:, g * HD : (g + 1) * HD].astype(jnp.float32) for g in range(GROUPS)]
    rows += [sk_ref[...].astype(jnp.float32), sv_ref[...].astype(jnp.float32)]
    qmsg[...] = jnp.concatenate(rows, axis=0).astype(jnp.bfloat16)

    pair = lax.broadcasted_iota(jnp.int32, (PAIRS, 1), 0)
    first = jnp.where(pair < PAIRS // 2, pool * PAIRS, other * PAIRS - PAIRS) + 2 * pair
    for conv in range(CONV):
        for side in range(2):
            found = jnp.max(
                jnp.where(slot_ref[conv : conv + 1, :] == first + side, 1.0, 0.0), axis=1, keepdims=True
            )
            bias[conv, :, side * HD : (side + 1) * HD] = jnp.broadcast_to(
                jnp.where(found > 0.5, 0.0, NEG), (PAIRS, HD)
            )

    pl.semaphore_wait(barrier, 2 * (CHIPS - 1) + 1 + 2 * tp)

    for step in range(CHIPS):
        to = chip_at(step) * 2 + home
        mine = qbuf.at[token]

        @pl.when(to != pool)
        def _():
            pltpu.make_async_remote_copy(
                src_ref=qmsg, dst_ref=mine, send_sem=send_sem.at[0], recv_sem=query_sem.at[token // TILE],
                device_id=(to, tp), device_id_type=MESH,
            ).start()

        @pl.when(to == pool)
        def _():
            pltpu.make_async_copy(qmsg, mine, query_sem.at[token // TILE]).start()

    for step in range(1, TP):

        @pl.when(tp - step >= 0)
        def _():
            for to in (pool, other):
                pl.semaphore_signal(ready_sem, inc=1, device_id=(to, tp - step), device_id_type=MESH)

    swaps = [
        pltpu.make_async_remote_copy(
            src_ref=src, dst_ref=dst, send_sem=part_send.at[n], recv_sem=part_recv.at[n],
            device_id=(other, tp), device_id_type=MESH,
        )
        for n, (src, dst) in enumerate(
            [
                (keys_ref, kbuf.at[pl.ds(PAIRS // 2, PAIRS // 2)]),
                (values_ref, vbuf.at[pl.ds(PAIRS // 2, PAIRS // 2)]),
                (w_ref, wbuf.at[core]),
                (qmsg, pmsg),
            ]
        )
    ]
    for copy in swaps[3:] + swaps[:3]:
        copy.start()
    for copy in local:
        copy.wait()
    for n in (3, 0, 1):
        swaps[n].wait()

    contract = (((1,), (1,)), ((), ()))

    def wait_bytes(ref, sem):
        pltpu.make_async_copy(ref, ref, sem).wait()

    tiles = (qmsg[...].astype(jnp.float32), pmsg[...].astype(jnp.float32))
    tiles = (jnp.where(core == 0, tiles[0], tiles[1]), jnp.where(core == 0, tiles[1], tiles[0]))
    blank = jnp.zeros((6, HD), jnp.float32)
    own_keys, own_values = [
        jnp.concatenate([tiles[0][row : row + 1], tiles[1][row : row + 1], blank], axis=0).astype(jnp.bfloat16)
        for row in (6, 7)
    ]
    own_pos = lax.rem(x, 2) * (SUF // 2) + 2 * y

    for group in GROUPED:
        conv = group[0] // (TILES // CONV)
        tokens = TILE * len(group)
        rows = GROUPS * tokens
        base = group[0] * TILE * 8
        here = pl.ds(base, tokens * 8)
        for tile in group:
            wait_bytes(qbuf.at[pl.ds(tile * TILE, TILE)], query_sem.at[tile])

        state[here, :] = qbuf[group[0] * TILE : group[0] * TILE + tokens].astype(jnp.float32).reshape(tokens * 8, HD)
        queries = jnp.concatenate(
            [state[pl.ds(base + g, tokens, stride=8), :] for g in range(GROUPS)], axis=0
        ).astype(jnp.bfloat16)
        top = jnp.full((rows, HD), NEG, jnp.float32)
        for r in range(PAIRS):
            s = lax.dot_general(queries, kbuf[r], contract, preferred_element_type=jnp.float32)
            s = s + bias[conv, r : r + 1, :]
            sbuf[r, 0:rows] = s
            top = jnp.maximum(top, jnp.maximum(s[:, :HD], s[:, HD:]))
        own = lax.dot_general(queries, own_keys, contract, preferred_element_type=jnp.float32)
        at = lax.rem(lax.broadcasted_iota(jnp.int32, (rows, 8), 0), tokens) + group[0] % 2 * TILE
        row_pos = (at // TILE * 2 + core) * TILE + at % TILE
        key = lax.broadcasted_iota(jnp.int32, (rows, 8), 1)
        own = jnp.where((key < 2) & (row_pos >= own_pos + key) & (x // 2 == conv), own, NEG)
        row_max = jnp.maximum(
            jnp.max(top, axis=1, keepdims=True), jnp.max(own, axis=1, keepdims=True)
        )
        row_max = row_max.astype(jnp.bfloat16).astype(jnp.float32)

        p = jnp.exp2((own - row_max) * EXP_SCALE)
        row_sum = jnp.sum(p, axis=1, keepdims=True)
        numer = jnp.dot(p.astype(jnp.bfloat16), own_values, preferred_element_type=jnp.float32)
        total = jnp.zeros((rows, HD), jnp.float32)
        for r in range(PAIRS):
            p = jnp.exp2((sbuf[r, 0:rows] - row_max) * EXP_SCALE)
            total = total + (p[:, :HD] + p[:, HD:])
            numer = numer + jnp.dot(p.astype(jnp.bfloat16), vbuf[r], preferred_element_type=jnp.float32)
        row_sum = row_sum + jnp.sum(total, axis=1, keepdims=True)

        lane = lax.broadcasted_iota(jnp.int32, (tokens, HD), 1)
        rounded = row_sum.astype(jnp.bfloat16).astype(jnp.float32)
        left = row_sum - rounded
        maxima = jnp.zeros((tokens, HD), jnp.float32)
        sums = jnp.zeros((tokens, HD), jnp.float32)
        for g in range(GROUPS):
            part = slice(g * tokens, (g + 1) * tokens)
            state[pl.ds(base + g, tokens, stride=8), :] = numer[part]
            maxima = jnp.where(lane == g, row_max[part], maxima)
            sums = jnp.where(lane == g, rounded[part], sums)
            sums = jnp.where(lane == g + HD // 2, left[part], sums)
        state[pl.ds(base + 6, tokens, stride=8), :] = maxima
        state[pl.ds(base + 7, tokens, stride=8), :] = sums
        smsg[here, :] = state[here, :].astype(jnp.bfloat16)

        my_tile = rbuf.at[conv, pl.ds(pl.multiple_of(chip * 16, 16), 16)]
        targets = [
            (to, couple)
            for couple in range(group[0] * TILE // 2, (group[-1] + 1) * TILE // 2)
            for to in owners(couple % CLASSES, conv)
        ]
        for to, couple in sorted(targets, key=lambda target: -hops_to_last(target[0])):
            couple_rows = smsg.at[pl.ds(couple * 16, 16)]

            @pl.when(chip != to)
            def _():
                pltpu.make_async_remote_copy(
                    src_ref=couple_rows, dst_ref=my_tile,
                    send_sem=send_sem.at[1 + 4 * conv], recv_sem=recv_sem.at[conv],
                    device_id=(to * 2 + core, tp), device_id_type=MESH,
                ).start()

            @pl.when(chip == to)
            def _():
                pltpu.make_async_copy(couple_rows, my_tile, recv_sem.at[conv]).start()

        if group == (0,):
            part = smsg.at[pl.ds(16, 48)]

            @pl.when((core == 0) & (chip != 0))
            def _():
                pltpu.make_async_remote_copy(
                    src_ref=part, dst_ref=fbuf.at[chip], send_sem=first_sem.at[0], recv_sem=first_sem.at[1],
                    device_id=(0, tp), device_id_type=MESH,
                ).start()

            @pl.when(pool == 0)
            def _():
                pltpu.make_async_copy(part, fbuf.at[0], first_sem.at[1]).start()

    mine = class_of(chip)

    def merge_couple(merged, which, conv):
        lane = lax.broadcasted_iota(jnp.int32, (1, HD), 1)
        limit = len_ref[:, conv : conv + 1]
        out_rows = []
        for half in range(2):

            def of_chips(row):
                return merged[pl.ds(half * 8 + row, CHIPS, stride=16), :]

            maxima = of_chips(6)
            sums = of_chips(7)
            sums = sums + pltpu.roll(sums, HD // 2, axis=1)
            best = jnp.max(maxima, axis=0, keepdims=True)
            scale = jnp.exp2((maxima - best) * EXP_SCALE)
            whole = jnp.sum(scale * sums, axis=0, keepdims=True)
            scale = scale / jnp.where(lane < GROUPS, whole, 1.0)
            position = (which // 4 * 2 + core) * TILE + which % 4 * 2 + half
            for g in range(GROUPS):
                row = jnp.sum(scale[:, g : g + 1] * of_chips(g), axis=0, keepdims=True)
                out_rows.append(jnp.where(limit > position, row, 0.0))
            out_rows.append(jnp.zeros((2, HD), jnp.float32))
        return jnp.concatenate(out_rows, axis=0).astype(jnp.bfloat16)

    def merge(conv):
        wait_bytes(rbuf.at[conv], recv_sem.at[conv])
        merged[0] = rbuf[conv].astype(jnp.float32)
        amsg[conv] = merge_couple(merged.at[0], mine, conv)

        my_couple = abuf.at[pl.ds(pl.multiple_of((conv * CLASSES + mine) * 16, 16), 16)]
        arrived = attend_sem.at[conv * 2 + mine // 4]
        for dx, dy in NEARER[conv]:
            to = row_of[dx] + place_of[dy]
            pltpu.make_async_remote_copy(
                src_ref=amsg.at[conv], dst_ref=my_couple, send_sem=send_sem.at[2 + 2 * conv], recv_sem=arrived,
                device_id=(to * 2 + core, tp), device_id_type=MESH,
            ).start()
        pltpu.make_async_copy(amsg.at[conv], my_couple, arrived).start()

    my_share = obuf.at[tp]

    def project(tile):
        here = pl.ds(tile * TILE * 8, TILE * 8)

        def arrived():
            wait_bytes(abuf.at[here], attend_sem.at[tile])
            state[here, :] = abuf[here, :].astype(jnp.float32)

        if tile == 0:
            pl.when(pool != 0)(arrived)

            @pl.when(pool == 0)
            def _():
                wait_bytes(fbuf, first_sem.at[1])
                state[0:16, :] = amsg[0].astype(jnp.float32)
                for which in range(1, 4):
                    states = fbuf[:, (which - 1) * 16 : which * 16, :]
                    merged[which] = states.astype(jnp.float32).reshape(CHIPS * 16, HD)
                for which in range(1, 4):
                    couple_rows = merge_couple(merged.at[which], which, 0)
                    state[which * 16 : (which + 1) * 16, :] = couple_rows.astype(jnp.float32)

        else:
            arrived()
        attention = jnp.concatenate(
            [state[pl.ds(tile * TILE * 8 + g, TILE, stride=8), :] for g in range(GROUPS)], axis=1
        ).astype(jnp.bfloat16)
        for side in (1, 0):
            share = lax.dot_general(attention, wbuf[side], contract, preferred_element_type=jnp.float32)
            rest = jnp.concatenate(
                [share[:, HD:], jnp.zeros((TILE, 2 * HD - share.shape[1]), jnp.float32)], axis=1
            )
            omsg[side, tile] = jnp.concatenate([share[:, :HD], rest], axis=0).astype(jnp.bfloat16)
            to = (chip * 2 + side, 2 * tile + core)
            stays = (to[0] == pool) & (to[1] == tp)

            @pl.when(jnp.logical_not(stays))
            def _():
                pltpu.make_async_remote_copy(
                    src_ref=omsg.at[side, tile], dst_ref=my_share,
                    send_sem=send_sem.at[3], recv_sem=recv_sem.at[2],
                    device_id=to, device_id_type=MESH,
                ).start()

            @pl.when(stays)
            def _():
                pltpu.make_async_copy(omsg.at[side, tile], my_share, recv_sem.at[2]).start()

    merge(0)
    swaps[2].wait()

    @pl.when(tp < TP - 1)
    def _():
        pl.semaphore_wait(ready_sem, 2 * (TP - 1 - tp))

    project(0)
    pl.when(x < NX // 2)(lambda: merge(1))
    project(1)
    project(2)
    project(3)

    wait_bytes(obuf, recv_sem.at[2])
    result = jnp.sum(obuf[...].astype(jnp.float32), axis=0)
    out_ref[:, :HD] = result[:TILE].astype(out_ref.dtype)
    out_ref[:, HD:] = result[TILE:, : out_ref.shape[1] - HD].astype(out_ref.dtype)

    @pl.when((core == 0) & (chip != 0))
    def _():
        wait_bytes(fbuf.at[0], first_sem.at[0])

    @pl.when(pool == 0)
    def _():
        wait_bytes(abuf.at[pl.ds(0, TILE * 8)], attend_sem.at[0])

    wait_bytes(rbuf.at[0, pl.ds(0, (CHIPS - 1) * 16)], send_sem.at[1])
    wait_bytes(abuf.at[pl.ds(0, len(NEARER[0]) * 16)], send_sem.at[2])

    @pl.when(x < NX // 2)
    def _():
        wait_bytes(rbuf.at[1, pl.ds(0, (CHIPS // 2 - 1) * 16)], send_sem.at[5])
        wait_bytes(abuf.at[pl.ds(0, len(NEARER[1]) * 16)], send_sem.at[4])

    @pl.when(x >= NX // 2)
    def _():
        wait_bytes(rbuf.at[1, pl.ds(0, CHIPS // 2 * 16)], send_sem.at[5])

    @pl.when(core == home)
    def _():
        wait_bytes(qbuf.at[pl.ds(0, CHIPS - 1)], send_sem.at[0])

    @pl.when(core != home)
    def _():
        wait_bytes(qbuf, send_sem.at[0])

    @pl.when(core == tp % 2)
    def _():
        wait_bytes(obuf.at[pl.ds(0, TP - 1)], send_sem.at[3])

    @pl.when(core != tp % 2)
    def _():
        wait_bytes(obuf, send_sem.at[3])


def shards(queries, suffix_keys, suffix_values, prefix_keys, prefix_values, block_slot, suffix_len, out_weight):
    f32, bf16 = jnp.float32, jnp.bfloat16
    columns = out_weight.shape[1]
    blocks = (PAIRS // 2, 2 * HD, HD)
    in_hbm = pl.BlockSpec(memory_space=pl.ANY)
    return pl.pallas_call(
        kernel,
        name="attend_and_project",
        out_shape=jax.ShapeDtypeStruct((8, columns), bf16),
        in_specs=[in_hbm] * 8,
        out_specs=pl.BlockSpec(memory_space=pltpu.VMEM),
        scratch_shapes=[
            pltpu.VMEM(queries.shape, bf16),
            pltpu.VMEM(suffix_keys.shape, bf16),
            pltpu.VMEM(suffix_values.shape, bf16),
            pltpu.VMEM(block_slot.shape, jnp.int32),
            pltpu.VMEM((1, CONV), jnp.int32),
            pltpu.VMEM((8, HD), bf16),
            pltpu.VMEM((8, HD), bf16),
            pltpu.VMEM((SUF, 8, HD), bf16),
            pltpu.VMEM((PAIRS, 2 * HD, HD), bf16),
            pltpu.VMEM((PAIRS, 2 * HD, HD), bf16),
            pltpu.VMEM((2, columns, GROUPS * HD), bf16),
            pltpu.VMEM((CONV, PAIRS, 2 * HD), f32),
            pltpu.VMEM((PAIRS, GROUPS * TILE * max(map(len, GROUPED)), 2 * HD), f32),
            pltpu.VMEM((SUF * 8, HD), f32),
            pltpu.VMEM((SUF * 8, HD), bf16),
            pltpu.VMEM((CONV, CHIPS * 16, HD), bf16),
            pltpu.VMEM((CHIPS, 48, HD), bf16),
            pltpu.VMEM((4, CHIPS * 16, HD), f32),
            pltpu.VMEM((CONV, 16, HD), bf16),
            pltpu.VMEM((SUF * 8, HD), bf16),
            pltpu.VMEM((2, TILES, 2 * TILE, HD), bf16),
            pltpu.VMEM((TP, 2 * TILE, HD), bf16),
            pltpu.SemaphoreType.DMA((5,)),
            pltpu.SemaphoreType.DMA((3,)),
            pltpu.SemaphoreType.DMA((4,)),
            pltpu.SemaphoreType.DMA((4,)),
            pltpu.SemaphoreType.DMA((TILES,)),
            pltpu.SemaphoreType.DMA((TILES,)),
            pltpu.SemaphoreType.DMA((6,)),
            pltpu.SemaphoreType.DMA((3,)),
            pltpu.SemaphoreType.DMA((2,)),
            pltpu.SemaphoreType.REGULAR,
        ],
        compiler_params=pltpu.CompilerParams(
            collective_id=0, has_side_effects=True, vmem_limit_bytes=55040 * 1024
        ),
    )(
        queries,
        suffix_keys,
        suffix_values,
        prefix_keys.reshape(blocks),
        prefix_values.reshape(blocks),
        block_slot,
        suffix_len.reshape(1, CONV),
        out_weight.T,
    )


def solution(mesh):
    in_specs = (
        P("pool", "tp"),
        P("pool", "tp"),
        P("pool", "tp"),
        P("pool", None, "tp"),
        P("pool", None, "tp"),
        P(),
        P(),
        P("tp", "pool"),
    )
    return jax.shard_map(shards, mesh=mesh, in_specs=in_specs, out_specs=P("tp", "pool"), check_vma=False)
```

```python
import functools
import math

import jax
import jax.numpy as jnp
from jax import lax
from jax.experimental import pallas as pl
from jax.experimental.pallas import tpu as pltpu
from jax.sharding import PartitionSpec as P

H = 48
KVH = 8
HD = 128
CONV = 2
SUF = 32
GROUPS = H // KVH
NEG = -(2.0**100)
EXP_SCALE = math.log2(math.e) / math.sqrt(HD)
MESH = pl.DeviceIdType.MESH

NX = 4
NY = 8
CHIPS = NX * NY
TP = 8
PAIRS = 16
TILE = 8
TILES = SUF // TILE
GROUPED = ((0,), (1,), (2,), (3,))


def far_first(count, step):
    half = count // 2
    return half + (1 - 2 * (step % 2)) * ((step + 1) // 2)


CLASSES = 8
NEARER = (
    ((2, 0), (1, 1), (1, 7), (1, 0), (3, 0), (0, 1), (0, 7)),
    (
        (2, 2), (3, 2), (1, 2), (2, 7), (2, 1), (0, 2), (3, 7), (3, 1),
        (2, 0), (1, 1), (1, 7), (1, 0), (3, 0), (0, 1), (0, 7),
    ),
)


def class_of(chip):
    return chip // NY % 2 * 4 + (chip % NY + 2 * (chip // (CHIPS // 2))) % 4


def owners(which, conv):
    return [chip for chip in range(CHIPS // (1 + conv)) if class_of(chip) == which]


LAST_X, LAST_Y = 2, 4


def hops_to_last(chip):
    return abs(chip // NY - LAST_X) + abs(chip % NY - LAST_Y)


def kernel(
    q_hbm, sk_hbm, sv_hbm, keys_ref, values_ref, slot_hbm, len_hbm, w_ref,
    out_ref,
    q_ref, sk_ref, sv_ref, slot_ref, len_ref,
    qmsg, pmsg, qbuf, kbuf, vbuf, wbuf, bias, sbuf, state, smsg, rbuf, fbuf, merged, amsg, abuf, omsg, obuf,
    small_sem, local_sem, part_send, part_recv, query_sem, attend_sem, send_sem, recv_sem, first_sem, ready_sem,
):
    pool = lax.axis_index("pool")
    tp = lax.axis_index("tp")
    core = lax.rem(pool, 2)
    chip = lax.div(pool, 2)
    x = lax.div(chip, NY)
    y = lax.rem(chip, NY)
    other = pool + 1 - 2 * core
    home = lax.div(y, NY // 2)
    token = x * TILE + lax.rem(y, NY // 2) * 2 + core

    row_of = [lax.rem(x + dx, NX) * NY for dx in range(NX)]
    place_of = [lax.rem(y + dy, NY) for dy in range(NY)]

    def chip_at(step):
        return row_of[far_first(NX, step % NX) % NX] + place_of[far_first(NY, step // NX) % NY]

    barrier = pltpu.get_barrier_semaphore()

    def greet(step, carry):
        to = chip_at(step)
        pl.semaphore_signal(barrier, inc=1, device_id=(to * 2 + core, tp), device_id_type=MESH)
        pl.semaphore_signal(barrier, inc=1, device_id=(to * 2 + 1 - core, tp), device_id_type=MESH)
        return carry

    for step in range(CHIPS - 1):
        greet(step, 0)

    for step in range(1, TP):

        @pl.when(tp + step < TP)
        def _():
            for to in (pool, other):
                pl.semaphore_signal(barrier, inc=1, device_id=(to, tp + step), device_id_type=MESH)

    pl.semaphore_signal(barrier, inc=1, device_id=(other, tp), device_id_type=MESH)

    small = [
        pltpu.make_async_copy(src, dst, small_sem.at[n])
        for n, (src, dst) in enumerate(
            [(q_hbm, q_ref), (sk_hbm, sk_ref), (sv_hbm, sv_ref), (slot_hbm, slot_ref), (len_hbm, len_ref)]
        )
    ]
    for copy in small:
        copy.start()
    local = [
        pltpu.make_async_copy(keys_ref, kbuf.at[pl.ds(0, PAIRS // 2)], local_sem.at[0]),
        pltpu.make_async_copy(values_ref, vbuf.at[pl.ds(0, PAIRS // 2)], local_sem.at[1]),
        pltpu.make_async_copy(w_ref, wbuf.at[core], local_sem.at[2]),
    ]
    for copy in local:
        copy.start()
    for copy in small:
        copy.wait()

    rows = [q_ref[:, g * HD : (g + 1) * HD].astype(jnp.float32) for g in range(GROUPS)]
    rows += [sk_ref[...].astype(jnp.float32), sv_ref[...].astype(jnp.float32)]
    qmsg[...] = jnp.concatenate(rows, axis=0).astype(jnp.bfloat16)

    pair = lax.broadcasted_iota(jnp.int32, (PAIRS, 1), 0)
    first = jnp.where(pair < PAIRS // 2, pool * PAIRS, other * PAIRS - PAIRS) + 2 * pair
    for conv in range(CONV):
        for side in range(2):
            found = jnp.max(
                jnp.where(slot_ref[conv : conv + 1, :] == first + side, 1.0, 0.0), axis=1, keepdims=True
            )
            bias[conv, :, side * HD : (side + 1) * HD] = jnp.broadcast_to(
                jnp.where(found > 0.5, 0.0, NEG), (PAIRS, HD)
            )

    pl.semaphore_wait(barrier, 2 * (CHIPS - 1) + 1 + 2 * tp)

    for step in range(CHIPS):
        to = chip_at(step) * 2 + home
        mine = qbuf.at[token]

        @pl.when(to != pool)
        def _():
            pltpu.make_async_remote_copy(
                src_ref=qmsg, dst_ref=mine, send_sem=send_sem.at[0], recv_sem=query_sem.at[token // TILE],
                device_id=(to, tp), device_id_type=MESH,
            ).start()

        @pl.when(to == pool)
        def _():
            pltpu.make_async_copy(qmsg, mine, query_sem.at[token // TILE]).start()

    for step in range(1, TP):

        @pl.when(tp - step >= 0)
        def _():
            for to in (pool, other):
                pl.semaphore_signal(ready_sem, inc=1, device_id=(to, tp - step), device_id_type=MESH)

    swaps = [
        pltpu.make_async_remote_copy(
            src_ref=src, dst_ref=dst, send_sem=part_send.at[n], recv_sem=part_recv.at[n],
            device_id=(other, tp), device_id_type=MESH,
        )
        for n, (src, dst) in enumerate(
            [
                (keys_ref, kbuf.at[pl.ds(PAIRS // 2, PAIRS // 2)]),
                (values_ref, vbuf.at[pl.ds(PAIRS // 2, PAIRS // 2)]),
                (w_ref, wbuf.at[core]),
                (qmsg, pmsg),
            ]
        )
    ]
    for copy in swaps[3:] + swaps[:3]:
        copy.start()
    for copy in local:
        copy.wait()
    for n in (3, 0, 1):
        swaps[n].wait()

    contract = (((1,), (1,)), ((), ()))

    def wait_bytes(ref, sem):
        pltpu.make_async_copy(ref, ref, sem).wait()

    tiles = (qmsg[...].astype(jnp.float32), pmsg[...].astype(jnp.float32))
    tiles = (jnp.where(core == 0, tiles[0], tiles[1]), jnp.where(core == 0, tiles[1], tiles[0]))
    blank = jnp.zeros((6, HD), jnp.float32)
    own_keys, own_values = [
        jnp.concatenate([tiles[0][row : row + 1], tiles[1][row : row + 1], blank], axis=0).astype(jnp.bfloat16)
        for row in (6, 7)
    ]
    own_pos = lax.rem(x, 2) * (SUF // 2) + 2 * y

    for group in GROUPED:
        conv = group[0] // (TILES // CONV)
        tokens = TILE * len(group)
        rows = GROUPS * tokens
        base = group[0] * TILE * 8
        here = pl.ds(base, tokens * 8)
        for tile in group:
            wait_bytes(qbuf.at[pl.ds(tile * TILE, TILE)], query_sem.at[tile])

        state[here, :] = qbuf[group[0] * TILE : group[0] * TILE + tokens].astype(jnp.float32).reshape(tokens * 8, HD)
        queries = jnp.concatenate(
            [state[pl.ds(base + g, tokens, stride=8), :] for g in range(GROUPS)], axis=0
        ).astype(jnp.bfloat16)
        top = jnp.full((rows, HD), NEG, jnp.float32)
        for r in range(PAIRS):
            s = lax.dot_general(queries, kbuf[r], contract, preferred_element_type=jnp.float32)
            s = s + bias[conv, r : r + 1, :]
            sbuf[r, 0:rows] = s
            top = jnp.maximum(top, jnp.maximum(s[:, :HD], s[:, HD:]))
        own = lax.dot_general(queries, own_keys, contract, preferred_element_type=jnp.float32)
        at = lax.rem(lax.broadcasted_iota(jnp.int32, (rows, 8), 0), tokens) + group[0] % 2 * TILE
        row_pos = (at // TILE * 2 + core) * TILE + at % TILE
        key = lax.broadcasted_iota(jnp.int32, (rows, 8), 1)
        own = jnp.where((key < 2) & (row_pos >= own_pos + key) & (x // 2 == conv), own, NEG)
        row_max = jnp.maximum(
            jnp.max(top, axis=1, keepdims=True), jnp.max(own, axis=1, keepdims=True)
        )
        row_max = row_max.astype(jnp.bfloat16).astype(jnp.float32)

        p = jnp.exp2((own - row_max) * EXP_SCALE)
        row_sum = jnp.sum(p, axis=1, keepdims=True)
        numer = jnp.dot(p.astype(jnp.bfloat16), own_values, preferred_element_type=jnp.float32)
        total = jnp.zeros((rows, HD), jnp.float32)
        for r in range(PAIRS):
            p = jnp.exp2((sbuf[r, 0:rows] - row_max) * EXP_SCALE)
            total = total + (p[:, :HD] + p[:, HD:])
            numer = numer + jnp.dot(p.astype(jnp.bfloat16), vbuf[r], preferred_element_type=jnp.float32)
        row_sum = row_sum + jnp.sum(total, axis=1, keepdims=True)

        lane = lax.broadcasted_iota(jnp.int32, (tokens, HD), 1)
        rounded = row_sum.astype(jnp.bfloat16).astype(jnp.float32)
        left = row_sum - rounded
        maxima = jnp.zeros((tokens, HD), jnp.float32)
        sums = jnp.zeros((tokens, HD), jnp.float32)
        for g in range(GROUPS):
            part = slice(g * tokens, (g + 1) * tokens)
            state[pl.ds(base + g, tokens, stride=8), :] = numer[part]
            maxima = jnp.where(lane == g, row_max[part], maxima)
            sums = jnp.where(lane == g, rounded[part], sums)
            sums = jnp.where(lane == g + HD // 2, left[part], sums)
        state[pl.ds(base + 6, tokens, stride=8), :] = maxima
        state[pl.ds(base + 7, tokens, stride=8), :] = sums
        smsg[here, :] = state[here, :].astype(jnp.bfloat16)

        my_tile = rbuf.at[conv, pl.ds(pl.multiple_of(chip * 16, 16), 16)]
        targets = [
            (to, couple)
            for couple in range(group[0] * TILE // 2, (group[-1] + 1) * TILE // 2)
            for to in owners(couple % CLASSES, conv)
        ]
        for to, couple in sorted(targets, key=lambda target: -hops_to_last(target[0])):
            couple_rows = smsg.at[pl.ds(couple * 16, 16)]

            @pl.when(chip != to)
            def _():
                pltpu.make_async_remote_copy(
                    src_ref=couple_rows, dst_ref=my_tile,
                    send_sem=send_sem.at[1 + 4 * conv], recv_sem=recv_sem.at[conv],
                    device_id=(to * 2 + core, tp), device_id_type=MESH,
                ).start()

            @pl.when(chip == to)
            def _():
                pltpu.make_async_copy(couple_rows, my_tile, recv_sem.at[conv]).start()

        if group == (0,):
            part = smsg.at[pl.ds(16, 48)]

            @pl.when((core == 0) & (chip != 0))
            def _():
                pltpu.make_async_remote_copy(
                    src_ref=part, dst_ref=fbuf.at[chip], send_sem=first_sem.at[0], recv_sem=first_sem.at[1],
                    device_id=(0, tp), device_id_type=MESH,
                ).start()

            @pl.when(pool == 0)
            def _():
                pltpu.make_async_copy(part, fbuf.at[0], first_sem.at[1]).start()

    mine = class_of(chip)

    def merge_couple(merged, which, conv):
        lane = lax.broadcasted_iota(jnp.int32, (1, HD), 1)
        limit = len_ref[:, conv : conv + 1]
        out_rows = []
        for half in range(2):

            def of_chips(row):
                return merged[pl.ds(half * 8 + row, CHIPS, stride=16), :]

            maxima = of_chips(6)
            sums = of_chips(7)
            sums = sums + pltpu.roll(sums, HD // 2, axis=1)
            best = jnp.max(maxima, axis=0, keepdims=True)
            scale = jnp.exp2((maxima - best) * EXP_SCALE)
            whole = jnp.sum(scale * sums, axis=0, keepdims=True)
            scale = scale / jnp.where(lane < GROUPS, whole, 1.0)
            position = (which // 4 * 2 + core) * TILE + which % 4 * 2 + half
            for g in range(GROUPS):
                row = jnp.sum(scale[:, g : g + 1] * of_chips(g), axis=0, keepdims=True)
                out_rows.append(jnp.where(limit > position, row, 0.0))
            out_rows.append(jnp.zeros((2, HD), jnp.float32))
        return jnp.concatenate(out_rows, axis=0).astype(jnp.bfloat16)

    def merge(conv):
        wait_bytes(rbuf.at[conv], recv_sem.at[conv])
        merged[0] = rbuf[conv].astype(jnp.float32)
        amsg[conv] = merge_couple(merged.at[0], mine, conv)

        my_couple = abuf.at[pl.ds(pl.multiple_of((conv * CLASSES + mine) * 16, 16), 16)]
        arrived = attend_sem.at[conv * 2 + mine // 4]
        for dx, dy in NEARER[conv]:
            to = row_of[dx] + place_of[dy]
            pltpu.make_async_remote_copy(
                src_ref=amsg.at[conv], dst_ref=my_couple, send_sem=send_sem.at[2 + 2 * conv], recv_sem=arrived,
                device_id=(to * 2 + core, tp), device_id_type=MESH,
            ).start()
        pltpu.make_async_copy(amsg.at[conv], my_couple, arrived).start()

    my_share = obuf.at[tp]

    def project(tile):
        here = pl.ds(tile * TILE * 8, TILE * 8)

        def arrived():
            wait_bytes(abuf.at[here], attend_sem.at[tile])
            state[here, :] = abuf[here, :].astype(jnp.float32)

        if tile == 0:
            pl.when(pool != 0)(arrived)

            @pl.when(pool == 0)
            def _():
                wait_bytes(fbuf, first_sem.at[1])
                state[0:16, :] = amsg[0].astype(jnp.float32)
                for which in range(1, 4):
                    states = fbuf[:, (which - 1) * 16 : which * 16, :]
                    merged[which] = states.astype(jnp.float32).reshape(CHIPS * 16, HD)
                for which in range(1, 4):
                    couple_rows = merge_couple(merged.at[which], which, 0)
                    state[which * 16 : (which + 1) * 16, :] = couple_rows.astype(jnp.float32)

        else:
            arrived()
        attention = jnp.concatenate(
            [state[pl.ds(tile * TILE * 8 + g, TILE, stride=8), :] for g in range(GROUPS)], axis=1
        ).astype(jnp.bfloat16)
        for side in (1, 0):
            share = lax.dot_general(attention, wbuf[side], contract, preferred_element_type=jnp.float32)
            rest = jnp.concatenate(
                [share[:, HD:], jnp.zeros((TILE, 2 * HD - share.shape[1]), jnp.float32)], axis=1
            )
            omsg[side, tile] = jnp.concatenate([share[:, :HD], rest], axis=0).astype(jnp.bfloat16)
            to = (chip * 2 + side, 2 * tile + core)
            stays = (to[0] == pool) & (to[1] == tp)

            @pl.when(jnp.logical_not(stays))
            def _():
                pltpu.make_async_remote_copy(
                    src_ref=omsg.at[side, tile], dst_ref=my_share,
                    send_sem=send_sem.at[3], recv_sem=recv_sem.at[2],
                    device_id=to, device_id_type=MESH,
                ).start()

            @pl.when(stays)
            def _():
                pltpu.make_async_copy(omsg.at[side, tile], my_share, recv_sem.at[2]).start()

    merge(0)
    swaps[2].wait()

    @pl.when(tp < TP - 1)
    def _():
        pl.semaphore_wait(ready_sem, 2 * (TP - 1 - tp))

    project(0)
    pl.when(x < NX // 2)(lambda: merge(1))
    project(1)
    project(2)
    project(3)

    wait_bytes(obuf, recv_sem.at[2])
    result = jnp.sum(obuf[...].astype(jnp.float32), axis=0)
    out_ref[:, :HD] = result[:TILE].astype(out_ref.dtype)
    out_ref[:, HD:] = result[TILE:, : out_ref.shape[1] - HD].astype(out_ref.dtype)

    @pl.when((core == 0) & (chip != 0))
    def _():
        wait_bytes(fbuf.at[0], first_sem.at[0])

    @pl.when(pool == 0)
    def _():
        wait_bytes(abuf.at[pl.ds(0, TILE * 8)], attend_sem.at[0])

    wait_bytes(rbuf.at[0, pl.ds(0, (CHIPS - 1) * 16)], send_sem.at[1])
    wait_bytes(abuf.at[pl.ds(0, len(NEARER[0]) * 16)], send_sem.at[2])

    @pl.when(x < NX // 2)
    def _():
        wait_bytes(rbuf.at[1, pl.ds(0, (CHIPS // 2 - 1) * 16)], send_sem.at[5])
        wait_bytes(abuf.at[pl.ds(0, len(NEARER[1]) * 16)], send_sem.at[4])

    @pl.when(x >= NX // 2)
    def _():
        wait_bytes(rbuf.at[1, pl.ds(0, CHIPS // 2 * 16)], send_sem.at[5])

    @pl.when(core == home)
    def _():
        wait_bytes(qbuf.at[pl.ds(0, CHIPS - 1)], send_sem.at[0])

    @pl.when(core != home)
    def _():
        wait_bytes(qbuf, send_sem.at[0])

    @pl.when(core == tp % 2)
    def _():
        wait_bytes(obuf.at[pl.ds(0, TP - 1)], send_sem.at[3])

    @pl.when(core != tp % 2)
    def _():
        wait_bytes(obuf, send_sem.at[3])


def shards(queries, suffix_keys, suffix_values, prefix_keys, prefix_values, block_slot, suffix_len, out_weight):
    f32, bf16 = jnp.float32, jnp.bfloat16
    columns = out_weight.shape[1]
    blocks = (PAIRS // 2, 2 * HD, HD)
    in_hbm = pl.BlockSpec(memory_space=pl.ANY)
    return pl.pallas_call(
        kernel,
        name="attend_and_project",
        out_shape=jax.ShapeDtypeStruct((8, columns), bf16),
        in_specs=[in_hbm] * 8,
        out_specs=pl.BlockSpec(memory_space=pltpu.VMEM),
        scratch_shapes=[
            pltpu.VMEM(queries.shape, bf16),
            pltpu.VMEM(suffix_keys.shape, bf16),
            pltpu.VMEM(suffix_values.shape, bf16),
            pltpu.VMEM(block_slot.shape, jnp.int32),
            pltpu.VMEM((1, CONV), jnp.int32),
            pltpu.VMEM((8, HD), bf16),
            pltpu.VMEM((8, HD), bf16),
            pltpu.VMEM((SUF, 8, HD), bf16),
            pltpu.VMEM((PAIRS, 2 * HD, HD), bf16),
            pltpu.VMEM((PAIRS, 2 * HD, HD), bf16),
            pltpu.VMEM((2, columns, GROUPS * HD), bf16),
            pltpu.VMEM((CONV, PAIRS, 2 * HD), f32),
            pltpu.VMEM((PAIRS, GROUPS * TILE * max(map(len, GROUPED)), 2 * HD), f32),
            pltpu.VMEM((SUF * 8, HD), f32),
            pltpu.VMEM((SUF * 8, HD), bf16),
            pltpu.VMEM((CONV, CHIPS * 16, HD), bf16),
            pltpu.VMEM((CHIPS, 48, HD), bf16),
            pltpu.VMEM((4, CHIPS * 16, HD), f32),
            pltpu.VMEM((CONV, 16, HD), bf16),
            pltpu.VMEM((SUF * 8, HD), bf16),
            pltpu.VMEM((2, TILES, 2 * TILE, HD), bf16),
            pltpu.VMEM((TP, 2 * TILE, HD), bf16),
            pltpu.SemaphoreType.DMA((5,)),
            pltpu.SemaphoreType.DMA((3,)),
            pltpu.SemaphoreType.DMA((4,)),
            pltpu.SemaphoreType.DMA((4,)),
            pltpu.SemaphoreType.DMA((TILES,)),
            pltpu.SemaphoreType.DMA((TILES,)),
            pltpu.SemaphoreType.DMA((6,)),
            pltpu.SemaphoreType.DMA((3,)),
            pltpu.SemaphoreType.DMA((2,)),
            pltpu.SemaphoreType.REGULAR,
        ],
        compiler_params=pltpu.CompilerParams(
            collective_id=0, has_side_effects=True, vmem_limit_bytes=55040 * 1024
        ),
    )(
        queries,
        suffix_keys,
        suffix_values,
        prefix_keys.reshape(blocks),
        prefix_values.reshape(blocks),
        block_slot,
        suffix_len.reshape(1, CONV),
        out_weight.T,
    )


def solution(mesh):
    in_specs = (
        P("pool", "tp"),
        P("pool", "tp"),
        P("pool", "tp"),
        P("pool", None, "tp"),
        P("pool", None, "tp"),
        P(),
        P(),
        P("tp", "pool"),
    )
    return jax.shard_map(shards, mesh=mesh, in_specs=in_specs, out_specs=P("tp", "pool"), check_vma=False)
```

```python
import functools
import math

import jax
import jax.numpy as jnp
from jax import lax
from jax.experimental import pallas as pl
from jax.experimental.pallas import tpu as pltpu
from jax.sharding import PartitionSpec as P

H = 48
KVH = 8
HD = 128
CONV = 2
SUF = 32
GROUPS = H // KVH
NEG = -(2.0**100)
EXP_SCALE = math.log2(math.e) / math.sqrt(HD)
MESH = pl.DeviceIdType.MESH

NX = 4
NY = 8
CHIPS = NX * NY
TP = 8
PAIRS = 16
TILE = 8
TILES = SUF // TILE
GROUPED = ((0,), (1,), (2,), (3,))


def far_first(count, step):
    half = count // 2
    return half + (1 - 2 * (step % 2)) * ((step + 1) // 2)


CLASSES = 8
NEARER = (
    ((2, 0), (1, 1), (1, 7), (1, 0), (3, 0), (0, 1), (0, 7)),
    (
        (2, 2), (3, 2), (1, 2), (2, 7), (2, 1), (0, 2), (3, 7), (3, 1),
        (2, 0), (1, 1), (1, 7), (1, 0), (3, 0), (0, 1), (0, 7),
    ),
)


def class_of(chip):
    return chip // NY % 2 * 4 + (chip % NY + 2 * (chip // (CHIPS // 2))) % 4


def owners(which, conv):
    return [chip for chip in range(CHIPS // (1 + conv)) if class_of(chip) == which]


LAST_X, LAST_Y = 2, 4


def hops_to_last(chip):
    return abs(chip // NY - LAST_X) + abs(chip % NY - LAST_Y)


def kernel(
    q_hbm, sk_hbm, sv_hbm, keys_ref, values_ref, slot_hbm, len_hbm, w_ref,
    out_ref,
    q_ref, sk_ref, sv_ref, slot_ref, len_ref,
    qmsg, pmsg, qbuf, kbuf, vbuf, wbuf, bias, sbuf, state, smsg, rbuf, fbuf, merged, amsg, abuf, omsg, obuf,
    small_sem, local_sem, part_send, part_recv, query_sem, attend_sem, send_sem, recv_sem, first_sem, ready_sem,
):
    pool = lax.axis_index("pool")
    tp = lax.axis_index("tp")
    core = lax.rem(pool, 2)
    chip = lax.div(pool, 2)
    x = lax.div(chip, NY)
    y = lax.rem(chip, NY)
    other = pool + 1 - 2 * core
    home = lax.div(y, NY // 2)
    token = x * TILE + lax.rem(y, NY // 2) * 2 + core

    row_of = [lax.rem(x + dx, NX) * NY for dx in range(NX)]
    place_of = [lax.rem(y + dy, NY) for dy in range(NY)]

    def chip_at(step):
        return row_of[far_first(NX, step % NX) % NX] + place_of[far_first(NY, step // NX) % NY]

    barrier = pltpu.get_barrier_semaphore()

    def greet(step, carry):
        to = chip_at(step)
        pl.semaphore_signal(barrier, inc=1, device_id=(to * 2 + core, tp), device_id_type=MESH)
        pl.semaphore_signal(barrier, inc=1, device_id=(to * 2 + 1 - core, tp), device_id_type=MESH)
        return carry

    for step in range(CHIPS - 1):
        greet(step, 0)

    for step in range(1, TP):

        @pl.when(tp + step < TP)
        def _():
            for to in (pool, other):
                pl.semaphore_signal(barrier, inc=1, device_id=(to, tp + step), device_id_type=MESH)

    pl.semaphore_signal(barrier, inc=1, device_id=(other, tp), device_id_type=MESH)

    small = [
        pltpu.make_async_copy(src, dst, small_sem.at[n])
        for n, (src, dst) in enumerate(
            [(q_hbm, q_ref), (sk_hbm, sk_ref), (sv_hbm, sv_ref), (slot_hbm, slot_ref), (len_hbm, len_ref)]
        )
    ]
    for copy in small:
        copy.start()
    local = [
        pltpu.make_async_copy(keys_ref, kbuf.at[pl.ds(0, PAIRS // 2)], local_sem.at[0]),
        pltpu.make_async_copy(values_ref, vbuf.at[pl.ds(0, PAIRS // 2)], local_sem.at[1]),
        pltpu.make_async_copy(w_ref, wbuf.at[core], local_sem.at[2]),
    ]
    for copy in local:
        copy.start()
    for copy in small:
        copy.wait()

    rows = [q_ref[:, g * HD : (g + 1) * HD].astype(jnp.float32) for g in range(GROUPS)]
    rows += [sk_ref[...].astype(jnp.float32), sv_ref[...].astype(jnp.float32)]
    qmsg[...] = jnp.concatenate(rows, axis=0).astype(jnp.bfloat16)

    pair = lax.broadcasted_iota(jnp.int32, (PAIRS, 1), 0)
    first = jnp.where(pair < PAIRS // 2, pool * PAIRS, other * PAIRS - PAIRS) + 2 * pair
    for conv in range(CONV):
        for side in range(2):
            found = jnp.max(
                jnp.where(slot_ref[conv : conv + 1, :] == first + side, 1.0, 0.0), axis=1, keepdims=True
            )
            bias[conv, :, side * HD : (side + 1) * HD] = jnp.broadcast_to(
                jnp.where(found > 0.5, 0.0, NEG), (PAIRS, HD)
            )

    pl.semaphore_wait(barrier, 2 * (CHIPS - 1) + 1 + 2 * tp)

    for step in range(CHIPS):
        to = chip_at(step) * 2 + home
        mine = qbuf.at[token]

        @pl.when(to != pool)
        def _():
            pltpu.make_async_remote_copy(
                src_ref=qmsg, dst_ref=mine, send_sem=send_sem.at[0], recv_sem=query_sem.at[token // TILE],
                device_id=(to, tp), device_id_type=MESH,
            ).start()

        @pl.when(to == pool)
        def _():
            pltpu.make_async_copy(qmsg, mine, query_sem.at[token // TILE]).start()

    for step in range(1, TP):

        @pl.when(tp - step >= 0)
        def _():
            for to in (pool, other):
                pl.semaphore_signal(ready_sem, inc=1, device_id=(to, tp - step), device_id_type=MESH)

    swaps = [
        pltpu.make_async_remote_copy(
            src_ref=src, dst_ref=dst, send_sem=part_send.at[n], recv_sem=part_recv.at[n],
            device_id=(other, tp), device_id_type=MESH,
        )
        for n, (src, dst) in enumerate(
            [
                (keys_ref, kbuf.at[pl.ds(PAIRS // 2, PAIRS // 2)]),
                (values_ref, vbuf.at[pl.ds(PAIRS // 2, PAIRS // 2)]),
                (w_ref, wbuf.at[core]),
                (qmsg, pmsg),
            ]
        )
    ]
    for copy in swaps[3:] + swaps[:3]:
        copy.start()
    for copy in local:
        copy.wait()
    for n in (3, 0, 1):
        swaps[n].wait()

    contract = (((1,), (1,)), ((), ()))

    def wait_bytes(ref, sem):
        pltpu.make_async_copy(ref, ref, sem).wait()

    tiles = (qmsg[...].astype(jnp.float32), pmsg[...].astype(jnp.float32))
    tiles = (jnp.where(core == 0, tiles[0], tiles[1]), jnp.where(core == 0, tiles[1], tiles[0]))
    blank = jnp.zeros((6, HD), jnp.float32)
    own_keys, own_values = [
        jnp.concatenate([tiles[0][row : row + 1], tiles[1][row : row + 1], blank], axis=0).astype(jnp.bfloat16)
        for row in (6, 7)
    ]
    own_pos = lax.rem(x, 2) * (SUF // 2) + 2 * y

    mine = class_of(chip)

    for group in GROUPED:
        conv = group[0] // (TILES // CONV)
        tokens = TILE * len(group)
        rows = GROUPS * tokens
        base = group[0] * TILE * 8
        here = pl.ds(base, tokens * 8)
        for tile in group:
            wait_bytes(qbuf.at[pl.ds(tile * TILE, TILE)], query_sem.at[tile])

        state[here, :] = qbuf[group[0] * TILE : group[0] * TILE + tokens].astype(jnp.float32).reshape(tokens * 8, HD)
        queries = jnp.concatenate(
            [state[pl.ds(base + g, tokens, stride=8), :] for g in range(GROUPS)], axis=0
        ).astype(jnp.bfloat16)
        top = jnp.full((rows, HD), NEG, jnp.float32)
        for r in range(PAIRS):
            s = lax.dot_general(queries, kbuf[r], contract, preferred_element_type=jnp.float32)
            s = s + bias[conv, r : r + 1, :]
            sbuf[r, 0:rows] = s
            top = jnp.maximum(top, jnp.maximum(s[:, :HD], s[:, HD:]))
        own = lax.dot_general(queries, own_keys, contract, preferred_element_type=jnp.float32)
        at = lax.rem(lax.broadcasted_iota(jnp.int32, (rows, 8), 0), tokens) + group[0] % 2 * TILE
        row_pos = (at // TILE * 2 + core) * TILE + at % TILE
        key = lax.broadcasted_iota(jnp.int32, (rows, 8), 1)
        own = jnp.where((key < 2) & (row_pos >= own_pos + key) & (x // 2 == conv), own, NEG)
        row_max = jnp.maximum(
            jnp.max(top, axis=1, keepdims=True), jnp.max(own, axis=1, keepdims=True)
        )
        row_max = row_max.astype(jnp.bfloat16).astype(jnp.float32)

        p = jnp.exp2((own - row_max) * EXP_SCALE)
        row_sum = jnp.sum(p, axis=1, keepdims=True)
        numer = jnp.dot(p.astype(jnp.bfloat16), own_values, preferred_element_type=jnp.float32)
        total = jnp.zeros((rows, HD), jnp.float32)
        for r in range(PAIRS):
            p = jnp.exp2((sbuf[r, 0:rows] - row_max) * EXP_SCALE)
            total = total + (p[:, :HD] + p[:, HD:])
            numer = numer + jnp.dot(p.astype(jnp.bfloat16), vbuf[r], preferred_element_type=jnp.float32)
        row_sum = row_sum + jnp.sum(total, axis=1, keepdims=True)

        lane = lax.broadcasted_iota(jnp.int32, (tokens, HD), 1)
        rounded = row_sum.astype(jnp.bfloat16).astype(jnp.float32)
        left = row_sum - rounded
        maxima = jnp.zeros((tokens, HD), jnp.float32)
        sums = jnp.zeros((tokens, HD), jnp.float32)
        for g in range(GROUPS):
            part = slice(g * tokens, (g + 1) * tokens)
            state[pl.ds(base + g, tokens, stride=8), :] = numer[part]
            maxima = jnp.where(lane == g, row_max[part], maxima)
            sums = jnp.where(lane == g, rounded[part], sums)
            sums = jnp.where(lane == g + HD // 2, left[part], sums)
        state[pl.ds(base + 6, tokens, stride=8), :] = maxima
        state[pl.ds(base + 7, tokens, stride=8), :] = sums
        smsg[here, :] = state[here, :].astype(jnp.bfloat16)

        my_tile = rbuf.at[conv, pl.ds(pl.multiple_of(chip * 16, 16), 16)]
        targets = [
            (to, couple)
            for couple in range(group[0] * TILE // 2, (group[-1] + 1) * TILE // 2)
            for to in owners(couple % CLASSES, conv)
        ]
        for to, couple in sorted(targets, key=lambda target: -hops_to_last(target[0])):

            @pl.when(chip != to)
            def _():
                pltpu.make_async_remote_copy(
                    src_ref=smsg.at[pl.ds(couple * 16, 16)], dst_ref=my_tile,
                    send_sem=send_sem.at[1 + 4 * conv], recv_sem=recv_sem.at[conv],
                    device_id=(to * 2 + core, tp), device_id_type=MESH,
                ).start()

        @pl.when((mine // 4 == group[0] % 2) & (x < NX // (1 + conv)))
        def _():
            own_rows = smsg.at[pl.ds(pl.multiple_of((conv * CLASSES + mine) * 16, 16), 16)]
            pltpu.make_async_copy(own_rows, my_tile, recv_sem.at[conv]).start()

        if group == (0,):
            part = smsg.at[pl.ds(16, 48)]

            @pl.when((core == 0) & (chip != 0))
            def _():
                pltpu.make_async_remote_copy(
                    src_ref=part, dst_ref=fbuf.at[chip], send_sem=first_sem.at[0], recv_sem=first_sem.at[1],
                    device_id=(0, tp), device_id_type=MESH,
                ).start()

            @pl.when(pool == 0)
            def _():
                pltpu.make_async_copy(part, fbuf.at[0], first_sem.at[1]).start()

    def merge_couple(merged, which, conv):
        lane = lax.broadcasted_iota(jnp.int32, (1, HD), 1)
        limit = len_ref[:, conv : conv + 1]
        out_rows = []
        for half in range(2):

            def of_chips(row):
                return merged[pl.ds(half * 8 + row, CHIPS, stride=16), :]

            maxima = of_chips(6)
            sums = of_chips(7)
            sums = sums + pltpu.roll(sums, HD // 2, axis=1)
            best = jnp.max(maxima, axis=0, keepdims=True)
            scale = jnp.exp2((maxima - best) * EXP_SCALE)
            whole = jnp.sum(scale * sums, axis=0, keepdims=True)
            scale = scale / jnp.where(lane < GROUPS, whole, 1.0)
            position = (which // 4 * 2 + core) * TILE + which % 4 * 2 + half
            for g in range(GROUPS):
                row = jnp.sum(scale[:, g : g + 1] * of_chips(g), axis=0, keepdims=True)
                out_rows.append(jnp.where(limit > position, row, 0.0))
            out_rows.append(jnp.zeros((2, HD), jnp.float32))
        return jnp.concatenate(out_rows, axis=0).astype(jnp.bfloat16)

    def merge(conv):
        wait_bytes(rbuf.at[conv], recv_sem.at[conv])
        merged[0, 0 : CHIPS * 16] = rbuf[conv].astype(jnp.float32)
        amsg[conv] = merge_couple(merged.at[0], mine, conv)

        my_couple = abuf.at[pl.ds(pl.multiple_of((conv * CLASSES + mine) * 16, 16), 16)]
        arrived = attend_sem.at[conv * 2 + mine // 4]
        for dx, dy in NEARER[conv]:
            to = row_of[dx] + place_of[dy]
            pltpu.make_async_remote_copy(
                src_ref=amsg.at[conv], dst_ref=my_couple, send_sem=send_sem.at[2 + 2 * conv], recv_sem=arrived,
                device_id=(to * 2 + core, tp), device_id_type=MESH,
            ).start()
        pltpu.make_async_copy(amsg.at[conv], my_couple, arrived).start()

    my_share = obuf.at[tp]

    def project(tile):
        here = pl.ds(tile * TILE * 8, TILE * 8)

        def arrived():
            wait_bytes(abuf.at[here], attend_sem.at[tile])
            state[here, :] = abuf[here, :].astype(jnp.float32)

        if tile == 0:
            pl.when(pool != 0)(arrived)

            @pl.when(pool == 0)
            def _():
                wait_bytes(fbuf, first_sem.at[1])
                state[0:16, :] = amsg[0].astype(jnp.float32)
                for which in range(1, 4):
                    states = fbuf[:, (which - 1) * 16 : which * 16, :]
                    merged[which, 0 : CHIPS * 16] = states.astype(jnp.float32).reshape(CHIPS * 16, HD)
                for which in range(1, 4):
                    couple_rows = merge_couple(merged.at[which], which, 0)
                    state[which * 16 : (which + 1) * 16, :] = couple_rows.astype(jnp.float32)

        else:
            arrived()
        attention = jnp.concatenate(
            [state[pl.ds(tile * TILE * 8 + g, TILE, stride=8), :] for g in range(GROUPS)], axis=1
        ).astype(jnp.bfloat16)
        for side in (1, 0):
            share = lax.dot_general(attention, wbuf[side], contract, preferred_element_type=jnp.float32)
            rest = jnp.concatenate(
                [share[:, HD:], jnp.zeros((TILE, 2 * HD - share.shape[1]), jnp.float32)], axis=1
            )
            omsg[side, tile] = jnp.concatenate([share[:, :HD], rest], axis=0).astype(jnp.bfloat16)
            to = (chip * 2 + side, 2 * tile + core)
            stays = (to[0] == pool) & (to[1] == tp)

            @pl.when(jnp.logical_not(stays))
            def _():
                pltpu.make_async_remote_copy(
                    src_ref=omsg.at[side, tile], dst_ref=my_share,
                    send_sem=send_sem.at[3], recv_sem=recv_sem.at[2],
                    device_id=to, device_id_type=MESH,
                ).start()

            @pl.when(stays)
            def _():
                pltpu.make_async_copy(omsg.at[side, tile], my_share, recv_sem.at[2]).start()

    merge(0)
    swaps[2].wait()

    @pl.when(tp < TP - 1)
    def _():
        pl.semaphore_wait(ready_sem, 2 * (TP - 1 - tp))

    project(0)
    pl.when(x < NX // 2)(lambda: merge(1))
    project(1)
    project(2)
    project(3)

    wait_bytes(obuf, recv_sem.at[2])
    result = jnp.sum(obuf[...].astype(jnp.float32), axis=0)
    out_ref[:, :HD] = result[:TILE].astype(out_ref.dtype)
    out_ref[:, HD:] = result[TILE:, : out_ref.shape[1] - HD].astype(out_ref.dtype)

    @pl.when((core == 0) & (chip != 0))
    def _():
        wait_bytes(fbuf.at[0], first_sem.at[0])

    @pl.when(pool == 0)
    def _():
        wait_bytes(abuf.at[pl.ds(0, TILE * 8)], attend_sem.at[0])

    wait_bytes(rbuf.at[0, pl.ds(0, (CHIPS - 1) * 16)], send_sem.at[1])
    wait_bytes(abuf.at[pl.ds(0, len(NEARER[0]) * 16)], send_sem.at[2])

    @pl.when(x < NX // 2)
    def _():
        wait_bytes(rbuf.at[1, pl.ds(0, (CHIPS // 2 - 1) * 16)], send_sem.at[5])
        wait_bytes(abuf.at[pl.ds(0, len(NEARER[1]) * 16)], send_sem.at[4])

    @pl.when(x >= NX // 2)
    def _():
        wait_bytes(rbuf.at[1, pl.ds(0, CHIPS // 2 * 16)], send_sem.at[5])

    @pl.when(core == home)
    def _():
        wait_bytes(qbuf.at[pl.ds(0, CHIPS - 1)], send_sem.at[0])

    @pl.when(core != home)
    def _():
        wait_bytes(qbuf, send_sem.at[0])

    @pl.when(core == tp % 2)
    def _():
        wait_bytes(obuf.at[pl.ds(0, TP - 1)], send_sem.at[3])

    @pl.when(core != tp % 2)
    def _():
        wait_bytes(obuf, send_sem.at[3])


def shards(queries, suffix_keys, suffix_values, prefix_keys, prefix_values, block_slot, suffix_len, out_weight):
    f32, bf16 = jnp.float32, jnp.bfloat16
    columns = out_weight.shape[1]
    blocks = (PAIRS // 2, 2 * HD, HD)
    in_hbm = pl.BlockSpec(memory_space=pl.ANY)
    return pl.pallas_call(
        kernel,
        name="attend_and_project",
        out_shape=jax.ShapeDtypeStruct((8, columns), bf16),
        in_specs=[in_hbm] * 8,
        out_specs=pl.BlockSpec(memory_space=pltpu.VMEM),
        scratch_shapes=[
            pltpu.VMEM(queries.shape, bf16),
            pltpu.VMEM(suffix_keys.shape, bf16),
            pltpu.VMEM(suffix_values.shape, bf16),
            pltpu.VMEM(block_slot.shape, jnp.int32),
            pltpu.VMEM((1, CONV), jnp.int32),
            pltpu.VMEM((8, HD), bf16),
            pltpu.VMEM((8, HD), bf16),
            pltpu.VMEM((SUF, 8, HD), bf16),
            pltpu.VMEM((PAIRS, 2 * HD, HD), bf16),
            pltpu.VMEM((PAIRS, 2 * HD, HD), bf16),
            pltpu.VMEM((2, columns, GROUPS * HD), bf16),
            pltpu.VMEM((CONV, PAIRS, 2 * HD), f32),
            pltpu.VMEM((PAIRS, GROUPS * TILE * max(map(len, GROUPED)), 2 * HD), f32),
            pltpu.VMEM((SUF * 8 + 8, HD), f32),
            pltpu.VMEM((SUF * 8, HD), bf16),
            pltpu.VMEM((CONV, CHIPS * 16, HD), bf16),
            pltpu.VMEM((CHIPS, 48, HD), bf16),
            pltpu.VMEM((4, CHIPS * 16 + 16, HD), f32),
            pltpu.VMEM((CONV, 16, HD), bf16),
            pltpu.VMEM((SUF * 8, HD), bf16),
            pltpu.VMEM((2, TILES, 2 * TILE, HD), bf16),
            pltpu.VMEM((TP, 2 * TILE, HD), bf16),
            pltpu.SemaphoreType.DMA((5,)),
            pltpu.SemaphoreType.DMA((3,)),
            pltpu.SemaphoreType.DMA((4,)),
            pltpu.SemaphoreType.DMA((4,)),
            pltpu.SemaphoreType.DMA((TILES,)),
            pltpu.SemaphoreType.DMA((TILES,)),
            pltpu.SemaphoreType.DMA((6,)),
            pltpu.SemaphoreType.DMA((3,)),
            pltpu.SemaphoreType.DMA((2,)),
            pltpu.SemaphoreType.REGULAR,
        ],
        compiler_params=pltpu.CompilerParams(
            collective_id=0, has_side_effects=True, vmem_limit_bytes=55040 * 1024
        ),
    )(
        queries,
        suffix_keys,
        suffix_values,
        prefix_keys.reshape(blocks),
        prefix_values.reshape(blocks),
        block_slot,
        suffix_len.reshape(1, CONV),
        out_weight.T,
    )


def solution(mesh):
    in_specs = (
        P("pool", "tp"),
        P("pool", "tp"),
        P("pool", "tp"),
        P("pool", None, "tp"),
        P("pool", None, "tp"),
        P(),
        P(),
        P("tp", "pool"),
    )
    return jax.shard_map(shards, mesh=mesh, in_specs=in_specs, out_specs=P("tp", "pool"), check_vma=False)
```
